512 devices in a mesh: lat: 128 (over x, z, y_hi), ch: 4 (over y_lo, core).
Axes of the slice: x: 4, y: 8 (y_hi: 4, y_lo: 2; y = y_hi * 2 + y_lo), z: 8, core: 2. Of those that a mesh axis runs over, the one named last changes fastest.
Arguments:
- tokens: bfloat16 [1, 256, 8, 69120], P(None, 'lat', 'ch'), may hold values from -6 to 6
- cotangent: bfloat16 [1, 256, 8, 69120], P(None, 'lat', 'ch'), may hold values from -6 to 6
- first_weight: bfloat16 [2, 8, 96, 96], P(None, 'ch'), may hold values from -0.4375 to 0.4375
- first_bias: bfloat16 [2, 8, 96], P(None, 'ch'), may hold values from -6 to 6
- second_weight: bfloat16 [2, 8, 96, 96], P(None, 'ch'), may hold values from -0.4375 to 0.4375
- relu_mask: int32 [1, 2, 8, 256, 24576], P(None, None, 'ch', 'lat'), may hold values 0 or 1
- shrink_mask: int32 [1, 2, 8, 256, 24576], P(None, None, 'ch', 'lat'), may hold values 0 or 1
Outputs:
- token_gradient: bfloat16 [1, 256, 8, 69120], P(None, 'lat', 'ch')
- first_gradient: float32 [2, 8, 96, 96], P(None, 'ch')
- bias_gradient: float32 [2, 8, 96], P(None, 'ch')
- second_gradient: float32 [2, 8, 96, 96], P(None, 'ch')
The draws below stay inside these ranges and needn't reach their ends.
All inputs are finite; a program needn't handle non-finite values. No bound on the sum of `relu_mask` or of `shrink_mask` on one device may be relied on, other than what follows from the above.
Results may differ from the reference program's by a relative error of at most 0.0093.
Values may be sent and summed in bfloat16 or wider, within the bound.
A program may use at most 64 MiB of HBM per device.

```python
import math
import jax
import jax.numpy as jnp
from jax import lax

BLOCKS = 8
BLOCK_SIZE = 96
NLON = 720
WAVES = 256
SAMPLES = 1
NLAT = 256


def plant(values, stream_key, least, top_value):
    place = [jax.random.randint(jax.random.fold_in(stream_key, axis), (), 0, length) for axis, length in enumerate(values.shape)]
    main_axis = values.shape.index(max(values.shape))
    beside = place[:main_axis] + [(place[main_axis] + 1) % values.shape[main_axis]] + place[main_axis + 1:]
    return values.at[tuple(place)].set(least).at[tuple(beside)].set(top_value)


def block_scale(stream_key, shape, cuts, least, largest):
    level, own = 1.0, jax.random.fold_in(stream_key, 6)
    for axis_at, shards_of in cuts:
        draws = jnp.exp(jax.random.uniform(jax.random.fold_in(own, axis_at), (shards_of,), jnp.float32, least / len(cuts), largest / len(cuts)))
        level = level * jnp.repeat(draws, shape[axis_at] // shards_of).reshape([-1 if axis == axis_at else 1 for axis in range(len(shape))])
    return level


def centred(key, shape, spread, reach, shards=(), kind=jnp.bfloat16):
    loudness = block_scale(key, shape, shards, -0.22, 0.18) if shards else 1.0
    result = jax.random.normal(key, shape, jnp.float32) * spread * loudness
    return jnp.minimum(jnp.maximum(result, -reach), reach).astype(kind)


def setup_inputs(seed: int = 0) -> dict:
    arg_keys = jax.random.split(jax.random.key(seed), 8)
    return {
        "tokens": centred(arg_keys[0], (SAMPLES, NLAT, BLOCKS, NLON * BLOCK_SIZE), 1.0, 6.0, ((1, 128), (2, 4))),
        "cotangent": centred(arg_keys[1], (SAMPLES, NLAT, BLOCKS, NLON * BLOCK_SIZE), 1.0, 6.0, ((1, 128), (2, 4))),
        "first_weight": centred(arg_keys[2], (2, BLOCKS, BLOCK_SIZE, BLOCK_SIZE), (2 * BLOCK_SIZE) ** -0.5, 0.4375, ((1, 4),)),
        "first_bias": centred(arg_keys[3], (2, BLOCKS, BLOCK_SIZE), 1.0, 6.0, ((1, 4),)),
        "second_weight": centred(arg_keys[4], (2, BLOCKS, BLOCK_SIZE, BLOCK_SIZE), (2 * BLOCK_SIZE) ** -0.5, 0.4375, ((1, 4),)),
        "relu_mask": plant((jax.random.randint(arg_keys[5], (SAMPLES, 2, BLOCKS, WAVES, NLAT * BLOCK_SIZE), 0, 2) < 1).astype(jnp.int32), jax.random.fold_in(arg_keys[5], 1), 0, 1),
        "shrink_mask": plant((jax.random.randint(arg_keys[6], (SAMPLES, 2, BLOCKS, WAVES, NLAT * BLOCK_SIZE), 0, 4) < 3).astype(jnp.int32), jax.random.fold_in(arg_keys[6], 1), 0, 1),
    }


def east_basis(count, waves):
    column = jnp.arange(count, dtype=jnp.int32)[:, None]
    number = jnp.arange(waves, dtype=jnp.int32)[None, :]
    phase = (column * number % count).astype(jnp.float32) * (2.0 * math.pi / count)
    factor = 1.0 / math.sqrt(count)
    return jnp.stack([jnp.cos(phase) * factor, -jnp.sin(phase) * factor], axis=1)

def north_basis(count):
    column = jnp.arange(count, dtype=jnp.int32)[:, None]
    number = jnp.arange(count, dtype=jnp.int32)[None, :]
    phase = (column * number % count).astype(jnp.float32) * (2.0 * math.pi / count)
    factor = 1.0 / math.sqrt(count)
    cosine = jnp.cos(phase) * factor
    sine = jnp.sin(phase) * factor
    upper = jnp.concatenate([cosine, sine], axis=1)
    lower = jnp.concatenate([-sine, cosine], axis=1)
    return jnp.concatenate([upper, lower], axis=0)

def complex_mix(left_real, left_imag, right_real, right_imag, form):
    left_real = left_real.astype(jnp.float32)
    left_imag = left_imag.astype(jnp.float32)
    right_real = right_real.astype(jnp.float32)
    right_imag = right_imag.astype(jnp.float32)
    real_part = jnp.einsum(form, left_real, right_real) - jnp.einsum(form, left_imag, right_imag)
    imag_part = jnp.einsum(form, left_real, right_imag) + jnp.einsum(form, left_imag, right_real)
    return (real_part, imag_part)

def reference(tokens, cotangent, first_weight, first_bias, second_weight, relu_mask, shrink_mask):
    east_table = east_basis(NLON, WAVES).astype(jnp.bfloat16).astype(jnp.float32)
    north_table = north_basis(NLAT).astype(jnp.bfloat16).astype(jnp.float32)
    factor = 1.0 / math.sqrt(NLAT * WAVES)

    def by_block(field):
        return jnp.moveaxis(field.reshape(SAMPLES, NLAT, BLOCKS, NLON, BLOCK_SIZE), 2, 0)

    def mask_block(mask):
        grid = jnp.moveaxis(mask.reshape(SAMPLES, 2, BLOCKS, WAVES, NLAT, BLOCK_SIZE), 2, 0)
        grid = jnp.swapaxes(grid, 3, 4)
        return grid.reshape(BLOCKS, SAMPLES, 2, NLAT * WAVES, BLOCK_SIZE)

    def to_modes(field):
        spec = jnp.einsum('bhwe,wsk->bshke', field.astype(jnp.float32), east_table).astype(jnp.bfloat16)
        flat = spec.reshape(SAMPLES, 2 * NLAT, WAVES * BLOCK_SIZE).astype(jnp.float32)
        mixed = jnp.einsum('qp,bpn->bqn', north_table, flat).astype(jnp.bfloat16)
        return mixed.reshape(SAMPLES, 2, NLAT * WAVES, BLOCK_SIZE)

    def one_block(item):
        field, upper_grad, relu_part, shrink_part, weight_one, bias_one, weight_two = item
        relu_keep = relu_part.astype(jnp.float32)
        modes = to_modes(field)
        upstream = to_modes(upper_grad) * shrink_part.astype(jnp.bfloat16)
        before_real, before_imag = complex_mix(modes[:, 0], modes[:, 1], weight_one[0], weight_one[1], 'bme,ef->bmf')
        hidden_real = (relu_keep[:, 0] * (before_real + bias_one[0].astype(jnp.float32))).astype(jnp.bfloat16)
        hidden_imag = (relu_keep[:, 1] * (before_imag + bias_one[1].astype(jnp.float32))).astype(jnp.bfloat16)
        second_real, second_imag = complex_mix(hidden_real, -hidden_imag, upstream[:, 0], upstream[:, 1], 'bme,bmf->ef')
        second_grad = jnp.stack([second_real, second_imag]) * factor
        back_real, back_imag = complex_mix(upstream[:, 0], upstream[:, 1], weight_two[0], -weight_two[1], 'bmf,ef->bme')
        inner_real = (relu_keep[:, 0] * back_real).astype(jnp.bfloat16)
        inner_imag = (relu_keep[:, 1] * back_imag).astype(jnp.bfloat16)
        first_real, first_imag = complex_mix(modes[:, 0], -modes[:, 1], inner_real, inner_imag, 'bme,bmf->ef')
        first_grad = jnp.stack([first_real, first_imag]) * factor
        bias_grad = jnp.stack([lax.optimization_barrier(jnp.sum(inner_real.astype(jnp.float32), axis=(0, 1))), lax.optimization_barrier(jnp.sum(inner_imag.astype(jnp.float32), axis=(0, 1)))]) * factor
        mode_real, mode_imag = complex_mix(inner_real, inner_imag, weight_one[0], -weight_one[1], 'bmf,ef->bme')
        stacked = jnp.stack([mode_real, mode_imag], axis=1).astype(jnp.bfloat16)
        stacked = stacked.reshape(SAMPLES, 2 * NLAT, WAVES * BLOCK_SIZE).astype(jnp.float32)
        returned = jnp.einsum('qp,bqn->bpn', north_table, stacked).astype(jnp.bfloat16)
        returned = returned.reshape(SAMPLES, 2, NLAT, WAVES, BLOCK_SIZE).astype(jnp.float32)
        token_grad = jnp.einsum('bshke,wsk->bhwe', returned, east_table) + upper_grad.astype(jnp.float32)
        return (token_grad.astype(jnp.bfloat16), first_grad, bias_grad, second_grad)
    items = (by_block(tokens), by_block(cotangent), mask_block(relu_mask), mask_block(shrink_mask), jnp.moveaxis(first_weight, 1, 0), jnp.moveaxis(first_bias, 1, 0), jnp.moveaxis(second_weight, 1, 0))
    token_all, first_all, bias_all, second_all = lax.map(one_block, items)
    token_gradient = jnp.moveaxis(token_all, 0, 2).reshape(SAMPLES, NLAT, BLOCKS, NLON * BLOCK_SIZE)
    return (token_gradient, jnp.moveaxis(first_all, 0, 1), jnp.moveaxis(bias_all, 0, 1), jnp.moveaxis(second_all, 0, 1))
```

```python
import functools
import math

import jax
import jax.numpy as jnp
import ml_dtypes
import numpy as np
from jax import lax
from jax.experimental import pallas as pl
from jax.experimental.pallas import tpu as pltpu
from jax.sharding import Mesh
from jax.sharding import PartitionSpec as P

MESH = pl.DeviceIdType.MESH
NAMES = ("lat_0", "lat_1", "lat_2")
WIDTH = 96
LANES = 128
ROWS = 192
GROUPS = 180
F32 = jnp.float32
BF16 = jnp.bfloat16
FIRST = (0, 96, 64, 32)


def tables(devices):
    nlat, nlon = (2 * devices, 4 * GROUPS)
    w = np.arange(nlon)[:, None]
    k = np.arange(2 * devices)[None, :]
    phase = (w * k % nlon) * (2.0 * math.pi / nlon)
    east = np.stack([np.cos(phase), -np.sin(phase)], axis=1) / math.sqrt(nlon)
    east = east.reshape(GROUPS, 4, 2, devices, 2).transpose(1, 0, 2, 3, 4)
    filled = np.zeros((4, ROWS, 2, devices, 2))
    filled[:, :GROUPS] = east
    out_east = filled.transpose(4, 2, 3, 0, 1).reshape(2, 2 * devices, 4 * ROWS)
    back = np.zeros((2, 2, 4, ROWS, devices, 2, 2))
    for h in range(2):
        back[h, :, :, :, :, :, h] = filled.transpose(4, 0, 1, 3, 2)
    back = back.reshape(2, 2, 4 * ROWS, 4 * devices)
    q = np.arange(nlat)[:, None]
    h = np.arange(nlat)[None, :]
    phase = (q * h % nlat) * (2.0 * math.pi / nlat)
    cosine, sine = (np.cos(phase) / math.sqrt(nlat), np.sin(phase) / math.sqrt(nlat))
    north = np.stack([np.stack([cosine, sine]), np.stack([-sine, cosine])])
    north = north.transpose(0, 2, 1, 3).reshape(2, nlat // 4, 4, 2, devices, 2)
    north = north.transpose(0, 2, 1, 4, 3, 5).reshape(2 * nlat, devices, 4)
    both = np.zeros((2, 2 * nlat, devices, 2, 4))
    for f in range(2):
        both[f, :, :, f] = north
    both = both.reshape(4 * nlat, 8 * devices)
    turned = north.reshape(2 * nlat, 4 * devices).T
    return tuple(
        np.ascontiguousarray(t.astype(np.float32).astype(ml_dtypes.bfloat16))
        for t in (out_east, both, turned, back)
    )


def lane_of(shape):
    return lax.broadcasted_iota(jnp.int32, shape, 1)


def moved(block, start, end):
    shift = (end - start) % LANES
    return block if shift == 0 else pltpu.roll(block, shift, 1)


def block_of(tiles, i):
    if i == 0:
        return tiles[0]
    if i == 3:
        return tiles[2]
    lane = lane_of(tiles[0].shape)
    return jnp.where(lane >= FIRST[i], tiles[i - 1], tiles[i])


def tiles_of(blocks):
    lane = lane_of(blocks[0].shape)
    return [jnp.where(lane < FIRST[i + 1], blocks[i], blocks[i + 1]) for i in range(3)]


def dot(a, b):
    return lax.dot_general(a, b, (((1,), (0,)), ((), ())), preferred_element_type=F32)


def dot_rows(a, b):
    return lax.dot_general(a, b, (((0,), (0,)), ((), ())), preferred_element_type=F32)


def dot_turned(a, b):
    return lax.dot_general(a, b, (((1,), (1,)), ((), ())), preferred_element_type=F32)


def kernel(
    sizes,
    per_owner,
    owners,
    tok,
    cot,
    w_one,
    b_one,
    w_two,
    relu,
    shrink,
    east_t,
    north_t,
    turned_t,
    back_t,
    out,
    first_out,
    bias_out,
    second_out,
    raw,
    spread,
    packed,
    wide,
    ready,
    arrived,
    stacked,
    masks,
    relu_f,
    shrink_f,
    weights,
    square,
    bias_row,
    modes,
    upstream,
    hidden,
    inner,
    grad_modes,
    leaving,
    returned,
    back_rows,
    own_sums,
    all_sums,
    shared,
    result,
    result_out,
    east_v,
    north_v,
    turned_v,
    back_v,
    w_one_v,
    b_one_v,
    w_two_v,
    load_sem,
    self_sem,
    send_sem,
    recv_sem,
    plane_sem,
):
    nx, nz, ny = sizes
    devices = nx * nz * ny
    nlat = 2 * devices
    quarter = nlat // 4
    cx, cz, cy = (lax.axis_index(n) for n in NAMES)
    me = (cx * nz + cz) * ny + cy

    def whom(x, z, y):
        return dict(zip(NAMES, (x, z, y)))

    def at_index(p):
        return whom(p // (nz * ny), lax.rem(p // ny, nz), lax.rem(p, ny))

    barrier = pltpu.get_barrier_semaphore()
    line = [whom(cx, lax.rem(cz + i, nz), cy) for i in range(1, nz)]
    plane = [
        whom(lax.rem(cx + i, nx), cz, lax.rem(cy + j, ny))
        for i in range(nx)
        for j in range(ny)
        if i or j
    ]
    for d in line + plane:
        pl.semaphore_signal(barrier, inc=1, device_id=d, device_id_type=MESH)

    loads = [
        pltpu.make_async_copy(src, dst, load_sem.at[i])
        for i, (src, dst) in enumerate(
            (
                (tok, raw.at[0]),
                (cot, raw.at[1]),
                (east_t, east_v),
                (relu, masks.at[0]),
                (shrink, masks.at[1]),
                (w_one, w_one_v),
                (b_one, b_one_v),
                (w_two, w_two_v),
                (north_t, north_v),
                (turned_t, turned_v),
                (back_t, back_v),
            )
        )
    ]
    for c in loads:
        c.start()

    lane = lane_of((ROWS, LANES))
    for i in range(4):
        spread[i, pl.ds(6 * GROUPS, 6 * (ROWS - GROUPS)), :] = jnp.zeros(
            (6 * (ROWS - GROUPS), LANES), F32
        )
    for f in range(2):
        loads[f].wait()
        for h in range(2):
            i = 2 * f + h
            spread[i, pl.ds(0, 6 * GROUPS), :] = raw[f, h].astype(F32)
            for j in range(4):
                b = [
                    block_of(
                        [spread[i, pl.ds(2 * c + n, ROWS, stride=6), :] for c in range(3)], j
                    )
                    for n in range(2)
                ]
                a0 = moved(b[0], FIRST[j], FIRST[0])
                a1 = moved(b[1], FIRST[j], FIRST[1])
                a2 = moved(b[0], FIRST[j], FIRST[2])
                a3 = moved(b[1], FIRST[j], FIRST[3])
                zero = jnp.zeros_like(a0)
                four = (
                    jnp.where(lane < 96, a0, a1),
                    jnp.where(lane < 64, a1, zero),
                    jnp.where(lane < 64, zero, a2),
                    jnp.where(lane < 32, a2, a3),
                )
                for t, v in enumerate(four):
                    packed[i, pl.ds(j * ROWS, ROWS), pl.ds(t * LANES, LANES)] = v.astype(BF16)
            if i == 0:
                loads[2].wait()
            for s in range(2):
                rows = pl.ds(s * devices, devices)
                even = dot(east_v[0, rows, :], packed[i, :, pl.ds(0, 256)])
                odd = dot(east_v[1, rows, :], packed[i, :, pl.ds(256, 256)])
                to = pl.ds(4 * f + 2 * s + h, devices, stride=8)
                wide[0, to, :] = even[:, :128]
                wide[1, to, :] = even[:, 128:] + odd[:, :128]
                wide[2, to, :] = odd[:, 128:]
        if f == 0:
            pl.semaphore_wait(barrier, len(line) + len(plane))
            for d in plane:
                pl.semaphore_signal(plane_sem, inc=1, device_id=d, device_id_type=MESH)
    for c in range(3):
        ready[:, :, pl.ds(c * LANES, LANES)] = wide[c].reshape(devices, 8, LANES).astype(BF16)
    pl.semaphore_wait(plane_sem, len(plane))

    def exchange(src, dst, n):
        def send(i, carry):
            p = lax.rem(me + i, devices)
            pltpu.make_async_remote_copy(
                src.at[pl.ds(p, 1)],
                dst.at[pl.ds(me, 1)],
                send_sem.at[n],
                recv_sem.at[n],
                device_id=at_index(p),
                device_id_type=MESH,
            ).start()
            return carry

        lax.fori_loop(1, devices, send, 0)
        own = pltpu.make_async_copy(src.at[pl.ds(me, 1)], dst.at[pl.ds(me, 1)], self_sem.at[n])
        own.start()
        many = pl.ds(0, devices - 1)
        whole = pltpu.make_async_remote_copy(
            src.at[many],
            dst.at[many],
            send_sem.at[n],
            recv_sem.at[n],
            device_id=whom(cx, lax.rem(cz + 1, nz), cy),
            device_id_type=MESH,
        )
        return own, whole

    own, whole = exchange(ready, arrived, 0)

    for c in loads[3:8]:
        c.wait()
    for m, to in ((0, relu_f), (1, shrink_f)):
        for s in range(2):
            for j in range(4):
                blocks = []
                for kn in range(4):
                    k, n = divmod(kn, 2)
                    three = [
                        masks[m, 2 * s + n, pl.ds(2 * c + k, quarter, stride=6), :]
                        for c in range(3)
                    ]
                    blocks.append(moved(block_of(three, j), FIRST[j], FIRST[kn]))
                for c, v in enumerate(tiles_of(blocks)):
                    to[pl.ds(s * nlat + j * quarter, quarter), pl.ds(c * LANES, LANES)] = v.astype(
                        F32
                    )
    square[...] = jnp.zeros_like(square)
    weights[...] = jnp.zeros_like(weights)
    column = lane_of((WIDTH, LANES))
    for m, src in ((0, w_one_v), (1, w_two_v)):
        for t in range(2):
            for n in range(2):
                square[:, pl.ds(0, WIDTH)] = src[t, n].astype(F32)
                base = square[...]
                for k in range(2):
                    kn = 2 * k + n
                    turned = moved(base, 0, FIRST[kn])
                    rows = pl.ds(kn * WIDTH, WIDTH)
                    if kn < 3:
                        keep = column >= FIRST[kn] if kn else column < WIDTH
                        c = (0, 0, 1)[kn]
                        weights[2 * m + t, rows, pl.ds(c * LANES, LANES)] = jnp.where(
                            keep, turned, 0.0
                        ).astype(BF16)
                    if kn > 0:
                        keep = column >= FIRST[3] if kn == 3 else column < FIRST[kn + 1]
                        c = (0, 1, 2, 2)[kn]
                        weights[2 * m + t, rows, pl.ds(c * LANES, LANES)] = jnp.where(
                            keep, turned, 0.0
                        ).astype(BF16)
    for t in range(2):
        for n in range(2):
            bias_row[pl.ds(2 * t + n, 1), pl.ds(0, WIDTH)] = b_one_v[t, pl.ds(n, 1), :].astype(F32)
    for t in range(2):
        blocks = [
            moved(
                jnp.broadcast_to(bias_row[pl.ds(2 * t + kn % 2, 1), pl.ds(0, LANES)], (8, LANES)),
                0,
                FIRST[kn],
            )
            for kn in range(4)
        ]
        for c, v in enumerate(tiles_of(blocks)):
            bias_row[pl.ds(8 + 8 * t, 8), pl.ds(c * LANES, LANES)] = v

    for c in loads[8:10]:
        c.wait()
    own.wait()
    whole.wait_recv()
    stacked[...] = arrived[...].reshape(8 * devices, 384)
    chunk = min(256, nlat)
    for f in (1, 0):
        for a in range(0, 2 * nlat, chunk):
            rows = pl.ds(a, chunk)
            value = dot(north_v[pl.ds(2 * f * nlat + a, chunk), :], stacked[...]).astype(BF16)
            if f:
                upstream[rows, :] = (value.astype(F32) * shrink_f[rows, :]).astype(BF16)
            else:
                modes[rows, :] = value

    half = min(128, nlat)
    parts = [(pl.ds(a, half), pl.ds(nlat + a, half)) for a in range(0, nlat, half)]

    def conjugate_mix(src, top, low, m):
        a, b = (src[top, :], src[low, :])
        real = dot_turned(a, weights[2 * m]) + dot_turned(b, weights[2 * m + 1])
        imag = dot_turned(b, weights[2 * m]) - dot_turned(a, weights[2 * m + 1])
        return real, imag

    for top, low in parts:
        real, imag = conjugate_mix(upstream, top, low, 1)
        inner[top, :] = (relu_f[top, :] * real).astype(BF16)
        inner[low, :] = (relu_f[low, :] * imag).astype(BF16)
    for top, low in parts:
        real, imag = conjugate_mix(inner, top, low, 0)
        grad_modes[top, :] = real.astype(BF16)
        grad_modes[low, :] = imag.astype(BF16)
    for a in range(0, 4 * devices, half):
        value = dot(turned_v[pl.ds(a, half), :], grad_modes[...]).astype(BF16)
        leaving[pl.ds(a // 4, half // 4)] = value.reshape(half // 4, 4, 384)

    own_back, whole_back = exchange(leaving, returned, 1)

    for top, low in parts:
        a, b = (modes[top, :], modes[low, :])
        real = dot(a, weights[0]) - dot(b, weights[1]) + bias_row[pl.ds(8, 1), :]
        imag = dot(a, weights[1]) + dot(b, weights[0]) + bias_row[pl.ds(16, 1), :]
        hidden[top, :] = (relu_f[top, :] * real).astype(BF16)
        hidden[low, :] = (relu_f[low, :] * imag).astype(BF16)
    upper, lower = (pl.ds(0, nlat), pl.ds(nlat, nlat))

    def diagonal(product, n):
        total = None
        for k in range(2):
            kn = 2 * k + n
            rows = product[kn * WIDTH : (kn + 1) * WIDTH]
            tiles = [rows[:, c * LANES : (c + 1) * LANES] for c in range(3)]
            block = moved(block_of(tiles, kn), FIRST[kn], 0)
            total = block if total is None else total + block
        return jnp.where(column < WIDTH, total, 0.0)

    eighth = WIDTH // 8
    for g, (left, right) in enumerate(((modes, inner), (hidden, upstream))):
        real = dot_rows(left[...], right[...])
        imag = dot_rows(left[upper, :], right[lower, :]) - dot_rows(left[lower, :], right[upper, :])
        for t, product in enumerate((real, imag)):
            for n in range(2):
                m = 4 * g + 2 * t + n
                shared[pl.ds(m * eighth, eighth)] = (
                    diagonal(product, n).reshape(eighth, 8, LANES).astype(BF16)
                )
    row8 = lax.broadcasted_iota(jnp.int32, (8, LANES), 0)
    total = jnp.zeros((8, LANES), F32)
    for t in range(2):
        sums = jnp.sum(inner[pl.ds(t * nlat, nlat), :].astype(F32), axis=0, keepdims=True)
        tiles = [
            jnp.broadcast_to(sums[:, c * LANES : (c + 1) * LANES], (8, LANES)) for c in range(3)
        ]
        for n in range(2):
            value = moved(block_of(tiles, n), FIRST[n], 0) + moved(
                block_of(tiles, 2 + n), FIRST[2 + n], 0
            )
            total = jnp.where(row8 == 2 * t + n, value, total)
    shared[8 * eighth] = total.astype(BF16)

    def to_owner(i, carry):
        p = lax.rem(me + i, devices)

        @pl.when(p < owners)
        def _():
            pltpu.make_async_remote_copy(
                shared.at[pl.ds(p * per_owner, per_owner)],
                own_sums.at[me],
                send_sem.at[2],
                recv_sem.at[2],
                device_id=at_index(p),
                device_id_type=MESH,
            ).start()

        return carry

    lax.fori_loop(1, devices, to_owner, 0)
    whole.wait_send()

    neighbour = whom(cx, lax.rem(cz + 1, nz), cy)

    def bytes_of(ref, n):
        return pltpu.make_async_remote_copy(
            ref,
            ref,
            send_sem.at[n],
            recv_sem.at[n],
            device_id=neighbour,
            device_id_type=MESH,
        )

    @pl.when(me < owners)
    def _():
        own_sums[me] = shared[pl.ds(me * per_owner, per_owner)]
        bytes_of(own_sums.at[pl.ds(0, devices - 1)], 2).wait_recv()
        all_sums[me] = jnp.sum(own_sums[...].astype(F32), axis=0).astype(BF16)

        def to_all(i, carry):
            pltpu.make_async_remote_copy(
                all_sums.at[me],
                all_sums.at[me],
                send_sem.at[3],
                recv_sem.at[3],
                device_id=at_index(lax.rem(me + i, devices)),
                device_id_type=MESH,
            ).start()
            return carry

        lax.fori_loop(1, devices, to_all, 0)

    loads[10].wait()
    own_back.wait()
    whole_back.wait_recv()
    back_rows[...] = returned[...].reshape(4 * devices, 384)
    for h in range(2):
        for j in range(4):
            rows = pl.ds(j * ROWS, ROWS)
            even = dot(back_v[h, 0, rows, :], back_rows[:, pl.ds(0, 256)])
            odd = dot(back_v[h, 1, rows, :], back_rows[:, pl.ds(128, 256)])
            tiles = (even[:, :128], even[:, 128:], None)
            parted = (None, odd[:, :128], odd[:, 128:])
            for n in range(2):
                value = moved(block_of(tiles, n), FIRST[n], FIRST[j]) + moved(
                    block_of(parted, 2 + n), FIRST[2 + n], FIRST[j]
                ) if n == 1 else moved(tiles[0], FIRST[0], FIRST[j]) + moved(
                    jnp.where(lane >= FIRST[2], parted[1], parted[2]), FIRST[2], FIRST[j]
                )
                result_out[j, n] = value
        for n in range(2):
            for c, v in enumerate(tiles_of([result_out[j, n] for j in range(4)])):
                result[h, pl.ds(2 * c + n, ROWS, stride=6), :] = v
        done = result[h, pl.ds(0, 6 * GROUPS), :] + raw[1, h].astype(F32)
        raw[0, h] = done.astype(BF16)
    store = pltpu.make_async_copy(raw.at[0], out, load_sem.at[0])
    store.start()

    whole_back.wait_send()

    @pl.when(me < owners)
    def _():
        bytes_of(shared.at[pl.ds(0, (owners - 1) * per_owner)], 2).wait_send()
        bytes_of(own_sums.at[pl.ds(0, devices - 1)], 3).wait_send()
        bytes_of(all_sums.at[pl.ds(0, owners - 1)], 3).wait_recv()

    @pl.when(me >= owners)
    def _():
        bytes_of(shared.at[pl.ds(0, owners * per_owner)], 2).wait_send()
        bytes_of(all_sums.at[pl.ds(0, owners)], 3).wait_recv()

    factor = 1.0 / math.sqrt(nlat * 2 * devices)
    sums = all_sums[...].reshape(owners * per_owner * 8, LANES)
    for g, ref in enumerate((first_out, second_out)):
        for t in range(2):
            for n in range(2):
                m = 4 * g + 2 * t + n
                ref[t, n] = sums[m * WIDTH : (m + 1) * WIDTH, :WIDTH].astype(F32) * factor
    last = sums[8 * WIDTH : 8 * WIDTH + 8].astype(F32) * factor
    for t in range(2):
        bias_out[t] = last[2 * t : 2 * t + 2, :WIDTH]
    store.wait()


def local(sizes, tokens, cotangent, first_weight, first_bias, second_weight, relu_mask, shrink_mask):
    devices = math.prod(sizes)
    nlat = 2 * devices
    blocks = 8 * WIDTH // 8 + 1
    per_owner = -(-blocks // devices)
    owners = -(-blocks // per_owner)

    def in_rows(field):
        return (
            field.reshape(2, 2, 3 * GROUPS, LANES)
            .transpose(0, 2, 1, 3)
            .reshape(2, 6 * GROUPS, LANES)
        )

    def mask_rows(mask):
        width = mask.shape[-1] // LANES
        return (
            mask.reshape(4, 2, width, LANES).transpose(0, 2, 1, 3).reshape(4, 2 * width, LANES)
        )

    constants = [jnp.asarray(t) for t in tables(devices)]
    anywhere = pl.BlockSpec(memory_space=pl.ANY)
    in_vmem = pl.BlockSpec(memory_space=pltpu.VMEM)

    def vmem(*shape, dtype=BF16):
        return pltpu.VMEM(shape, dtype)

    out, first, bias, second = pl.pallas_call(
        functools.partial(kernel, sizes, per_owner, owners),
        out_shape=(
            jax.ShapeDtypeStruct((2, 6 * GROUPS, LANES), BF16),
            jax.ShapeDtypeStruct(first_weight.shape, F32),
            jax.ShapeDtypeStruct(first_bias.shape, F32),
            jax.ShapeDtypeStruct(second_weight.shape, F32),
        ),
        in_specs=[anywhere] * 11,
        out_specs=(anywhere, in_vmem, in_vmem, in_vmem),
        scratch_shapes=[
            vmem(2, 2, 6 * GROUPS, LANES),
            vmem(4, 6 * ROWS, LANES, dtype=F32),
            vmem(4, 4 * ROWS, 4 * LANES),
            vmem(3, 8 * devices, LANES, dtype=F32),
            vmem(devices, 8, 384),
            vmem(devices, 8, 384),
            vmem(8 * devices, 384),
            vmem(2, 4, 6 * (nlat // 4), LANES, dtype=jnp.int32),
            vmem(2 * nlat, 384, dtype=F32),
            vmem(2 * nlat, 384, dtype=F32),
            vmem(4, 384, 384),
            vmem(WIDTH, LANES, dtype=F32),
            vmem(24, 384, dtype=F32),
            vmem(2 * nlat, 384),
            vmem(2 * nlat, 384),
            vmem(2 * nlat, 384),
            vmem(2 * nlat, 384),
            vmem(2 * nlat, 384),
            vmem(devices, 4, 384),
            vmem(devices, 4, 384),
            vmem(4 * devices, 384),
            vmem(devices, per_owner, 8, LANES),
            vmem(owners, per_owner, 8, LANES),
            vmem(owners * per_owner, 8, LANES),
            vmem(2, 6 * ROWS, LANES, dtype=F32),
            vmem(4, 2, ROWS, LANES, dtype=F32),
            vmem(*constants[0].shape),
            vmem(*constants[1].shape),
            vmem(*constants[2].shape),
            vmem(*constants[3].shape),
            vmem(*first_weight.shape),
            vmem(*first_bias.shape),
            vmem(*second_weight.shape),
            pltpu.SemaphoreType.DMA((11,)),
            pltpu.SemaphoreType.DMA((2,)),
            pltpu.SemaphoreType.DMA((4,)),
            pltpu.SemaphoreType.DMA((4,)),
            pltpu.SemaphoreType.REGULAR,
        ],
        compiler_params=pltpu.CompilerParams(
            collective_id=0, has_side_effects=True, vmem_limit_bytes=48 * 1024 * 1024
        ),
    )(
        in_rows(tokens),
        in_rows(cotangent),
        first_weight,
        first_bias,
        second_weight,
        mask_rows(relu_mask),
        mask_rows(shrink_mask),
        *constants,
    )
    token_gradient = (
        out.reshape(2, 3 * GROUPS, 2, LANES).transpose(0, 2, 1, 3).reshape(tokens.shape)
    )
    return (token_gradient, first, bias, second)


def solution(mesh, sizes=(4, 8, 4)):
    finer = Mesh(mesh.devices.reshape(*sizes, mesh.shape["ch"]), (*NAMES, "ch"))
    in_specs = (
        P(None, NAMES, "ch", None),
        P(None, NAMES, "ch", None),
        P(None, "ch", None, None),
        P(None, "ch", None),
        P(None, "ch", None, None),
        P(None, None, "ch", NAMES, None),
        P(None, None, "ch", NAMES, None),
    )
    out_specs = (
        P(None, NAMES, "ch", None),
        P(None, "ch", None, None),
        P(None, "ch", None),
        P(None, "ch", None, None),
    )
    return jax.shard_map(
        functools.partial(local, sizes),
        mesh=finer,
        in_specs=in_specs,
        out_specs=out_specs,
        check_vma=False,
    )
```

```python
import functools
import math

import jax
import jax.numpy as jnp
import ml_dtypes
import numpy as np
from jax import lax
from jax.experimental import pallas as pl
from jax.experimental.layout import Layout, with_layout_constraint
from jax.experimental.pallas import tpu as pltpu
from jax.sharding import Mesh
from jax.sharding import PartitionSpec as P

MESH = pl.DeviceIdType.MESH
NAMES = ("lat_0", "lat_1", "lat_2")
WIDTH = 96
LANES = 128
ROWS = 192
GROUPS = 180
F32 = jnp.float32
BF16 = jnp.bfloat16
FIRST = (0, 96, 64, 32)


def tables(devices):
    nlat, nlon = (2 * devices, 4 * GROUPS)
    w = np.arange(nlon)[:, None]
    k = np.arange(2 * devices)[None, :]
    phase = (w * k % nlon) * (2.0 * math.pi / nlon)
    east = np.stack([np.cos(phase), -np.sin(phase)], axis=1) / math.sqrt(nlon)
    east = east.reshape(GROUPS, 4, 2, devices, 2).transpose(1, 0, 2, 3, 4)
    filled = np.zeros((4, ROWS, 2, devices, 2))
    filled[:, :GROUPS] = east
    out_east = filled.transpose(4, 2, 3, 0, 1).reshape(2, 2 * devices, 4 * ROWS)
    back = np.zeros((2, 2, 4, ROWS, devices, 2, 2))
    for h in range(2):
        back[h, :, :, :, :, :, h] = filled.transpose(4, 0, 1, 3, 2)
    back = back.reshape(2, 2, 4 * ROWS, 4 * devices)
    q = np.arange(nlat)[:, None]
    h = np.arange(nlat)[None, :]
    phase = (q * h % nlat) * (2.0 * math.pi / nlat)
    cosine, sine = (np.cos(phase) / math.sqrt(nlat), np.sin(phase) / math.sqrt(nlat))
    north = np.stack([np.stack([cosine, sine]), np.stack([-sine, cosine])])
    north = north.transpose(0, 2, 1, 3).reshape(2, nlat // 4, 4, 2, devices, 2)
    north = north.transpose(0, 2, 1, 4, 3, 5).reshape(2 * nlat, devices, 4)
    both = np.zeros((2, 2 * nlat, devices, 2, 4))
    for f in range(2):
        both[f, :, :, f] = north
    both = both.reshape(4 * nlat, 8 * devices)
    turned = north.reshape(2 * nlat, 4 * devices).T
    return tuple(
        np.ascontiguousarray(t.astype(np.float32).astype(ml_dtypes.bfloat16))
        for t in (out_east, both, turned, back)
    )


def lane_of(shape):
    return lax.broadcasted_iota(jnp.int32, shape, 1)


def moved(block, start, end):
    shift = (end - start) % LANES
    return block if shift == 0 else pltpu.roll(block, shift, 1)


def block_of(tiles, i):
    if i == 0:
        return tiles[0]
    if i == 3:
        return tiles[2]
    lane = lane_of(tiles[0].shape)
    return jnp.where(lane >= FIRST[i], tiles[i - 1], tiles[i])


def tiles_of(blocks):
    lane = lane_of(blocks[0].shape)
    return [jnp.where(lane < FIRST[i + 1], blocks[i], blocks[i + 1]) for i in range(3)]


def dot(a, b):
    return lax.dot_general(a, b, (((1,), (0,)), ((), ())), preferred_element_type=F32)


def dot_rows(a, b):
    return lax.dot_general(a, b, (((0,), (0,)), ((), ())), preferred_element_type=F32)


def dot_turned(a, b):
    return lax.dot_general(a, b, (((1,), (1,)), ((), ())), preferred_element_type=F32)


def kernel(
    sizes,
    per_owner,
    owners,
    tok,
    cot,
    w_one,
    b_one,
    w_two,
    relu,
    shrink,
    east_t,
    north_t,
    turned_t,
    back_t,
    out,
    all_sums,
    raw,
    spread,
    packed,
    wide,
    ready,
    arrived,
    stacked,
    masks,
    relu_f,
    shrink_f,
    weights,
    square,
    bias_row,
    modes,
    upstream,
    hidden,
    inner,
    grad_modes,
    leaving,
    returned,
    back_rows,
    own_sums,
    shared,
    result,
    result_out,
    east_v,
    north_v,
    turned_v,
    back_v,
    w_one_v,
    b_one_v,
    w_two_v,
    load_sem,
    self_sem,
    send_sem,
    recv_sem,
):
    nx, nz, ny = sizes
    devices = nx * nz * ny
    nlat = 2 * devices
    quarter = nlat // 4
    cx, cz, cy = (lax.axis_index(n) for n in NAMES)
    me = (cx * nz + cz) * ny + cy

    def whom(x, z, y):
        return dict(zip(NAMES, (x, z, y)))

    def at_index(p):
        return whom(p // (nz * ny), lax.rem(p // ny, nz), lax.rem(p, ny))

    barrier = pltpu.get_barrier_semaphore()

    def greet(i, carry):
        d = at_index(lax.rem(me + i, devices))
        pl.semaphore_signal(barrier, inc=1, device_id=d, device_id_type=MESH)
        return carry

    loads = [
        pltpu.make_async_copy(src, dst, load_sem.at[i])
        for i, (src, dst) in enumerate(
            (
                (tok, raw.at[0]),
                (cot, raw.at[1]),
                (east_t, east_v),
                (relu, masks.at[0]),
                (shrink, masks.at[1]),
                (w_one, w_one_v),
                (b_one, b_one_v),
                (w_two, w_two_v),
                (north_t, north_v),
                (turned_t, turned_v),
                (back_t, back_v),
            )
        )
    ]
    for c in loads:
        c.start()
    lax.fori_loop(1, devices, greet, 0)

    lane = lane_of((ROWS, LANES))
    for i in range(4):
        spread[i, pl.ds(6 * GROUPS, 6 * (ROWS - GROUPS)), :] = jnp.zeros(
            (6 * (ROWS - GROUPS), LANES), F32
        )
    for f in range(2):
        loads[f].wait()
        for h in range(2):
            i = 2 * f + h
            spread[i, pl.ds(0, 6 * GROUPS), :] = raw[f, h].astype(F32)
            for j in range(4):
                b = [
                    block_of(
                        [spread[i, pl.ds(2 * c + n, ROWS, stride=6), :] for c in range(3)], j
                    )
                    for n in range(2)
                ]
                a0 = moved(b[0], FIRST[j], FIRST[0])
                a1 = moved(b[1], FIRST[j], FIRST[1])
                a2 = moved(b[0], FIRST[j], FIRST[2])
                a3 = moved(b[1], FIRST[j], FIRST[3])
                zero = jnp.zeros_like(a0)
                four = (
                    jnp.where(lane < 96, a0, a1),
                    jnp.where(lane < 64, a1, zero),
                    jnp.where(lane < 64, zero, a2),
                    jnp.where(lane < 32, a2, a3),
                )
                for t, v in enumerate(four):
                    packed[i, pl.ds(j * ROWS, ROWS), pl.ds(t * LANES, LANES)] = v.astype(BF16)
            if i == 0:
                loads[2].wait()
            for s in range(2):
                rows = pl.ds(s * devices, devices)
                even = dot(east_v[0, rows, :], packed[i, :, pl.ds(0, 256)])
                odd = dot(east_v[1, rows, :], packed[i, :, pl.ds(256, 256)])
                to = pl.ds(4 * f + 2 * s + h, devices, stride=8)
                wide[0, to, :] = even[:, :128]
                wide[1, to, :] = even[:, 128:] + odd[:, :128]
                wide[2, to, :] = odd[:, 128:]
    for c in range(3):
        ready[:, :, pl.ds(c * LANES, LANES)] = wide[c].reshape(devices, 8, LANES).astype(BF16)
    pl.semaphore_wait(barrier, devices - 1)

    def exchange(src, dst, n):
        def send(i, carry):
            p = lax.rem(me + i, devices)
            pltpu.make_async_remote_copy(
                src.at[pl.ds(p, 1)],
                dst.at[pl.ds(me, 1)],
                send_sem.at[n],
                recv_sem.at[n],
                device_id=at_index(p),
                device_id_type=MESH,
            ).start()
            return carry

        lax.fori_loop(1, devices, send, 0)
        own = pltpu.make_async_copy(src.at[pl.ds(me, 1)], dst.at[pl.ds(me, 1)], self_sem.at[n])
        own.start()
        many = pl.ds(0, devices - 1)
        whole = pltpu.make_async_remote_copy(
            src.at[many],
            dst.at[many],
            send_sem.at[n],
            recv_sem.at[n],
            device_id=whom(cx, lax.rem(cz + 1, nz), cy),
            device_id_type=MESH,
        )
        return own, whole

    own, whole = exchange(ready, arrived, 0)

    for c in loads[3:8]:
        c.wait()
    for m, to in ((0, relu_f), (1, shrink_f)):
        for s in range(2):
            for j in range(4):
                blocks = []
                for kn in range(4):
                    k, n = divmod(kn, 2)
                    three = [
                        masks[m, 2 * s + n, pl.ds(2 * c + k, quarter, stride=6), :]
                        for c in range(3)
                    ]
                    blocks.append(moved(block_of(three, j), FIRST[j], FIRST[kn]))
                for c, v in enumerate(tiles_of(blocks)):
                    to[pl.ds(s * nlat + j * quarter, quarter), pl.ds(c * LANES, LANES)] = v.astype(
                        F32
                    )
    square[...] = jnp.zeros_like(square)
    weights[...] = jnp.zeros_like(weights)
    column = lane_of((WIDTH, LANES))
    for m, src in ((0, w_one_v), (1, w_two_v)):
        for t in range(2):
            for n in range(2):
                square[:, pl.ds(0, WIDTH)] = src[t, n].astype(F32)
                base = square[...]
                for k in range(2):
                    kn = 2 * k + n
                    turned = moved(base, 0, FIRST[kn])
                    rows = pl.ds(kn * WIDTH, WIDTH)
                    if kn < 3:
                        keep = column >= FIRST[kn] if kn else column < WIDTH
                        c = (0, 0, 1)[kn]
                        weights[2 * m + t, rows, pl.ds(c * LANES, LANES)] = jnp.where(
                            keep, turned, 0.0
                        ).astype(BF16)
                    if kn > 0:
                        keep = column >= FIRST[3] if kn == 3 else column < FIRST[kn + 1]
                        c = (0, 1, 2, 2)[kn]
                        weights[2 * m + t, rows, pl.ds(c * LANES, LANES)] = jnp.where(
                            keep, turned, 0.0
                        ).astype(BF16)
    for t in range(2):
        for n in range(2):
            bias_row[pl.ds(2 * t + n, 1), pl.ds(0, WIDTH)] = b_one_v[t, pl.ds(n, 1), :].astype(F32)
    for t in range(2):
        blocks = [
            moved(
                jnp.broadcast_to(bias_row[pl.ds(2 * t + kn % 2, 1), pl.ds(0, LANES)], (8, LANES)),
                0,
                FIRST[kn],
            )
            for kn in range(4)
        ]
        for c, v in enumerate(tiles_of(blocks)):
            bias_row[pl.ds(8 + 8 * t, 8), pl.ds(c * LANES, LANES)] = v

    for c in loads[8:10]:
        c.wait()
    own.wait()
    whole.wait_recv()
    stacked[...] = arrived[...].reshape(8 * devices, 384)
    chunk = min(256, nlat)
    for f in (1, 0):
        for a in range(0, 2 * nlat, chunk):
            rows = pl.ds(a, chunk)
            value = dot(north_v[pl.ds(2 * f * nlat + a, chunk), :], stacked[...]).astype(BF16)
            if f:
                upstream[rows, :] = (value.astype(F32) * shrink_f[rows, :]).astype(BF16)
            else:
                modes[rows, :] = value

    half = min(128, nlat)
    parts = [(pl.ds(a, half), pl.ds(nlat + a, half)) for a in range(0, nlat, half)]

    def conjugate_mix(src, top, low, m):
        a, b = (src[top, :], src[low, :])
        real = dot_turned(a, weights[2 * m]) + dot_turned(b, weights[2 * m + 1])
        imag = dot_turned(b, weights[2 * m]) - dot_turned(a, weights[2 * m + 1])
        return real, imag

    for top, low in parts:
        real, imag = conjugate_mix(upstream, top, low, 1)
        inner[top, :] = (relu_f[top, :] * real).astype(BF16)
        inner[low, :] = (relu_f[low, :] * imag).astype(BF16)
    for top, low in parts:
        a, b = (modes[top, :], modes[low, :])
        real = dot(a, weights[0]) - dot(b, weights[1]) + bias_row[pl.ds(8, 1), :]
        imag = dot(a, weights[1]) + dot(b, weights[0]) + bias_row[pl.ds(16, 1), :]
        hidden[top, :] = (relu_f[top, :] * real).astype(BF16)
        hidden[low, :] = (relu_f[low, :] * imag).astype(BF16)
    upper, lower = (pl.ds(0, nlat), pl.ds(nlat, nlat))

    def diagonal(product, n, start):
        total = None
        for k in range(2):
            kn = 2 * k + n
            rows = product[kn * WIDTH : (kn + 1) * WIDTH]
            tiles = [rows[:, c * LANES : (c + 1) * LANES] for c in range(3)]
            block = moved(block_of(tiles, kn), FIRST[kn], start)
            total = block if total is None else total + block
        return total

    eighth = WIDTH // 8
    for g, (left, right) in enumerate(((modes, inner), (hidden, upstream))):
        real = dot_rows(left[...], right[...])
        imag = dot_rows(left[upper, :], right[lower, :]) - dot_rows(left[lower, :], right[upper, :])
        blocks = [
            diagonal(product, n, FIRST[2 * t + n])
            for t, product in enumerate((real, imag))
            for n in range(2)
        ]
        for c, v in enumerate(tiles_of(blocks)):
            shared[pl.ds((3 * g + c) * eighth, eighth)] = v.reshape(eighth, 8, LANES).astype(BF16)
    row8 = lax.broadcasted_iota(jnp.int32, (8, LANES), 0)
    total = jnp.zeros((8, LANES), F32)
    for t in range(2):
        sums = jnp.sum(inner[pl.ds(t * nlat, nlat), :].astype(F32), axis=0, keepdims=True)
        tiles = [
            jnp.broadcast_to(sums[:, c * LANES : (c + 1) * LANES], (8, LANES)) for c in range(3)
        ]
        for n in range(2):
            value = moved(block_of(tiles, n), FIRST[n], 0) + moved(
                block_of(tiles, 2 + n), FIRST[2 + n], 0
            )
            total = jnp.where(row8 == 2 * t + n, value, total)
    shared[6 * eighth] = total.astype(BF16)

    def to_owner(i, carry):
        p = lax.rem(me + i, owners)

        @pl.when(p != me)
        def _():
            pltpu.make_async_remote_copy(
                shared.at[pl.ds(p * per_owner, per_owner)],
                own_sums.at[me],
                send_sem.at[2],
                recv_sem.at[2],
                device_id=at_index(p),
                device_id_type=MESH,
            ).start()

        return carry

    lax.fori_loop(0, owners, to_owner, 0)
    whole.wait_send()

    for top, low in parts:
        real, imag = conjugate_mix(inner, top, low, 0)
        grad_modes[top, :] = real.astype(BF16)
        grad_modes[low, :] = imag.astype(BF16)
    for a in range(0, 4 * devices, half):
        value = dot(turned_v[pl.ds(a, half), :], grad_modes[...]).astype(BF16)
        leaving[pl.ds(a // 4, half // 4)] = value.reshape(half // 4, 4, 384)

    own_back, whole_back = exchange(leaving, returned, 1)

    neighbour = whom(cx, lax.rem(cz + 1, nz), cy)

    def bytes_of(ref, n):
        return pltpu.make_async_remote_copy(
            ref,
            ref,
            send_sem.at[n],
            recv_sem.at[n],
            device_id=neighbour,
            device_id_type=MESH,
        )

    @pl.when(me < owners)
    def _():
        own_sums[me] = shared[pl.ds(me * per_owner, per_owner)]
        bytes_of(own_sums.at[pl.ds(0, devices - 1)], 2).wait_recv()
        all_sums[me] = jnp.sum(own_sums[...].astype(F32), axis=0).astype(BF16)

        def to_all(i, carry):
            pltpu.make_async_remote_copy(
                all_sums.at[me],
                all_sums.at[me],
                send_sem.at[3],
                recv_sem.at[3],
                device_id=at_index(lax.rem(me + i, devices)),
                device_id_type=MESH,
            ).start()
            return carry

        lax.fori_loop(1, devices, to_all, 0)

    loads[10].wait()
    own_back.wait()
    whole_back.wait_recv()
    back_rows[...] = returned[...].reshape(4 * devices, 384)
    for h in range(2):
        for j in range(4):
            rows = pl.ds(j * ROWS, ROWS)
            even = dot(back_v[h, 0, rows, :], back_rows[:, pl.ds(0, 256)])
            odd = dot(back_v[h, 1, rows, :], back_rows[:, pl.ds(128, 256)])
            tiles = (even[:, :128], even[:, 128:], None)
            parted = (None, odd[:, :128], odd[:, 128:])
            for n in range(2):
                value = moved(block_of(tiles, n), FIRST[n], FIRST[j]) + moved(
                    block_of(parted, 2 + n), FIRST[2 + n], FIRST[j]
                ) if n == 1 else moved(tiles[0], FIRST[0], FIRST[j]) + moved(
                    jnp.where(lane >= FIRST[2], parted[1], parted[2]), FIRST[2], FIRST[j]
                )
                result_out[j, n] = value
        for n in range(2):
            for c, v in enumerate(tiles_of([result_out[j, n] for j in range(4)])):
                result[h, pl.ds(2 * c + n, ROWS, stride=6), :] = v
        done = result[h, pl.ds(0, 6 * GROUPS), :] + raw[1, h].astype(F32)
        out[h] = done.astype(BF16)

    whole_back.wait_send()

    @pl.when(me < owners)
    def _():
        bytes_of(shared.at[pl.ds(0, (owners - 1) * per_owner)], 2).wait_send()
        bytes_of(own_sums.at[pl.ds(0, devices - 1)], 3).wait_send()
        bytes_of(all_sums.at[pl.ds(0, owners - 1)], 3).wait_recv()

    @pl.when(me >= owners)
    def _():
        bytes_of(shared.at[pl.ds(0, owners * per_owner)], 2).wait_send()
        bytes_of(all_sums.at[pl.ds(0, owners)], 3).wait_recv()


def finish(factor, ahead, sums, out, first_out, bias_out, second_out, sem):
    store = pltpu.make_async_copy(ahead, out, sem)
    store.start()
    eighth = WIDTH // 8
    for g, ref in enumerate((first_out, second_out)):
        tiles = [
            sums[pl.ds((3 * g + c) * eighth, eighth)].reshape(WIDTH, LANES).astype(F32)
            for c in range(3)
        ]
        for t in range(2):
            for n in range(2):
                i = 2 * t + n
                block = moved(block_of(tiles, i), FIRST[i], 0)
                ref[t, n] = block[:, :WIDTH] * factor
    last = sums[6 * eighth].astype(F32) * factor
    for t in range(2):
        bias_out[t] = last[2 * t : 2 * t + 2, :WIDTH]
    store.wait()


def local(sizes, tokens, cotangent, first_weight, first_bias, second_weight, relu_mask, shrink_mask):
    devices = math.prod(sizes)
    nlat = 2 * devices
    blocks = 6 * WIDTH // 8 + 1
    per_owner = -(-blocks // devices)
    owners = -(-blocks // per_owner)

    pairs = Layout(major_to_minor=(0, 2, 1, 3))

    def in_rows(field):
        tiles = with_layout_constraint(field.reshape(2, 2, 3 * GROUPS, LANES), pairs)
        return tiles.transpose(0, 2, 1, 3).reshape(2, 6 * GROUPS, LANES)

    def mask_rows(mask):
        width = mask.shape[-1] // LANES
        return (
            mask.reshape(4, 2, width, LANES).transpose(0, 2, 1, 3).reshape(4, 2 * width, LANES)
        )

    constants = [jnp.asarray(t) for t in tables(devices)]
    anywhere = pl.BlockSpec(memory_space=pl.ANY)
    in_vmem = pl.BlockSpec(memory_space=pltpu.VMEM)

    def vmem(*shape, dtype=BF16):
        return pltpu.VMEM(shape, dtype)

    ahead, sums = pl.pallas_call(
        functools.partial(kernel, sizes, per_owner, owners),
        out_shape=(
            jax.ShapeDtypeStruct((2, 6 * GROUPS, LANES), BF16),
            jax.ShapeDtypeStruct((owners, per_owner, 8, LANES), BF16),
        ),
        in_specs=[anywhere] * 11,
        out_specs=(in_vmem, in_vmem),
        scratch_shapes=[
            vmem(2, 2, 6 * GROUPS, LANES),
            vmem(4, 6 * ROWS, LANES, dtype=F32),
            vmem(4, 4 * ROWS, 4 * LANES),
            vmem(3, 8 * devices, LANES, dtype=F32),
            vmem(devices, 8, 384),
            vmem(devices, 8, 384),
            vmem(8 * devices, 384),
            vmem(2, 4, 6 * (nlat // 4), LANES, dtype=jnp.int32),
            vmem(2 * nlat, 384, dtype=F32),
            vmem(2 * nlat, 384, dtype=F32),
            vmem(4, 384, 384),
            vmem(WIDTH, LANES, dtype=F32),
            vmem(24, 384, dtype=F32),
            vmem(2 * nlat, 384),
            vmem(2 * nlat, 384),
            vmem(2 * nlat, 384),
            vmem(2 * nlat, 384),
            vmem(2 * nlat, 384),
            vmem(devices, 4, 384),
            vmem(devices, 4, 384),
            vmem(4 * devices, 384),
            vmem(devices, per_owner, 8, LANES),
            vmem(owners * per_owner, 8, LANES),
            vmem(2, 6 * ROWS, LANES, dtype=F32),
            vmem(4, 2, ROWS, LANES, dtype=F32),
            vmem(*constants[0].shape),
            vmem(*constants[1].shape),
            vmem(*constants[2].shape),
            vmem(*constants[3].shape),
            vmem(*first_weight.shape),
            vmem(*first_bias.shape),
            vmem(*second_weight.shape),
            pltpu.SemaphoreType.DMA((11,)),
            pltpu.SemaphoreType.DMA((2,)),
            pltpu.SemaphoreType.DMA((4,)),
            pltpu.SemaphoreType.DMA((4,)),
        ],
        compiler_params=pltpu.CompilerParams(
            collective_id=0, has_side_effects=True, vmem_limit_bytes=60 * 1024 * 1024
        ),
    )(
        in_rows(tokens),
        in_rows(cotangent),
        first_weight,
        first_bias,
        second_weight,
        mask_rows(relu_mask),
        mask_rows(shrink_mask),
        *constants,
    )
    out, first, bias, second = pl.pallas_call(
        functools.partial(finish, 1.0 / math.sqrt(nlat * 2 * devices)),
        out_shape=(
            jax.ShapeDtypeStruct((2, 6 * GROUPS, LANES), BF16),
            jax.ShapeDtypeStruct(first_weight.shape, F32),
            jax.ShapeDtypeStruct(first_bias.shape, F32),
            jax.ShapeDtypeStruct(second_weight.shape, F32),
        ),
        in_specs=(in_vmem, in_vmem),
        out_specs=(anywhere, in_vmem, in_vmem, in_vmem),
        scratch_shapes=[pltpu.SemaphoreType.DMA],
    )(ahead, sums.reshape(owners * per_owner, 8, LANES))
    out = out.reshape(2, 3 * GROUPS, 2, LANES).transpose(0, 2, 1, 3)
    token_gradient = with_layout_constraint(out, pairs).reshape(tokens.shape)
    return (token_gradient, first, bias, second)


def solution(mesh, sizes=(4, 8, 4)):
    finer = Mesh(mesh.devices.reshape(*sizes, mesh.shape["ch"]), (*NAMES, "ch"))
    in_specs = (
        P(None, NAMES, "ch", None),
        P(None, NAMES, "ch", None),
        P(None, "ch", None, None),
        P(None, "ch", None),
        P(None, "ch", None, None),
        P(None, None, "ch", NAMES, None),
        P(None, None, "ch", NAMES, None),
    )
    out_specs = (
        P(None, NAMES, "ch", None),
        P(None, "ch", None, None),
        P(None, "ch", None),
        P(None, "ch", None, None),
    )
    return jax.shard_map(
        functools.partial(local, sizes),
        mesh=finer,
        in_specs=in_specs,
        out_specs=out_specs,
        check_vma=False,
    )
```

```python
import functools
import math

import jax
import jax.numpy as jnp
import ml_dtypes
import numpy as np
from jax import lax
from jax.experimental import pallas as pl
from jax.experimental.layout import Layout, with_layout_constraint
from jax.experimental.pallas import tpu as pltpu
from jax.sharding import Mesh
from jax.sharding import PartitionSpec as P

MESH = pl.DeviceIdType.MESH
NAMES = ("lat_0", "lat_1", "lat_2")
WIDTH = 96
LANES = 128
STEP = 7
ROWS = 192
GROUPS = 180
F32 = jnp.float32
BF16 = jnp.bfloat16
FIRST = (0, 96, 64, 32)


def tables(devices):
    nlat, nlon = (2 * devices, 4 * GROUPS)
    w = np.arange(nlon)[:, None]
    k = np.arange(2 * devices)[None, :]
    phase = (w * k % nlon) * (2.0 * math.pi / nlon)
    east = np.stack([np.cos(phase), -np.sin(phase)], axis=1) / math.sqrt(nlon)
    east = east.reshape(GROUPS, 4, 2, devices, 2).transpose(1, 0, 2, 3, 4)
    filled = np.zeros((4, ROWS, 2, devices, 2))
    filled[:, :GROUPS] = east
    out_east = filled.transpose(4, 2, 3, 0, 1).reshape(2, 2 * devices, 4 * ROWS)
    back = np.zeros((2, 2, 4, ROWS, devices, 2, 2))
    for h in range(2):
        back[h, :, :, :, :, :, h] = filled.transpose(4, 0, 1, 3, 2)
    back = back.reshape(2, 2, 4 * ROWS, 4 * devices)
    q = np.arange(nlat)[:, None]
    h = np.arange(nlat)[None, :]
    phase = (q * h % nlat) * (2.0 * math.pi / nlat)
    cosine, sine = (np.cos(phase) / math.sqrt(nlat), np.sin(phase) / math.sqrt(nlat))
    north = np.stack([np.stack([cosine, sine]), np.stack([-sine, cosine])])
    north = north.transpose(0, 2, 1, 3).reshape(2, nlat // 4, 4, 2, devices, 2)
    north = north.transpose(0, 2, 1, 4, 3, 5).reshape(2 * nlat, devices, 4)
    both = np.zeros((2, 2 * nlat, devices, 2, 4))
    for f in range(2):
        both[f, :, :, f] = north
    both = both.reshape(4 * nlat, 8 * devices)
    turned = north.reshape(2 * nlat, 4 * devices).T
    return tuple(
        np.ascontiguousarray(t.astype(np.float32).astype(ml_dtypes.bfloat16))
        for t in (out_east, both, turned, back)
    )


def lane_of(shape):
    return lax.broadcasted_iota(jnp.int32, shape, 1)


def moved(block, start, end):
    shift = (end - start) % LANES
    return block if shift == 0 else pltpu.roll(block, shift, 1)


def block_of(tiles, i):
    if i == 0:
        return tiles[0]
    if i == 3:
        return tiles[2]
    lane = lane_of(tiles[0].shape)
    return jnp.where(lane >= FIRST[i], tiles[i - 1], tiles[i])


def tiles_of(blocks):
    lane = lane_of(blocks[0].shape)
    return [jnp.where(lane < FIRST[i + 1], blocks[i], blocks[i + 1]) for i in range(3)]


def dot(a, b):
    return lax.dot_general(a, b, (((1,), (0,)), ((), ())), preferred_element_type=F32)


def dot_rows(a, b):
    return lax.dot_general(a, b, (((0,), (0,)), ((), ())), preferred_element_type=F32)


def dot_turned(a, b):
    return lax.dot_general(a, b, (((1,), (1,)), ((), ())), preferred_element_type=F32)


def kernel(
    sizes,
    per_owner,
    owners,
    tok,
    cot,
    w_one,
    b_one,
    w_two,
    relu,
    shrink,
    east_t,
    north_t,
    turned_t,
    back_t,
    out,
    all_sums,
    raw,
    spread,
    packed,
    wide,
    ready,
    arrived,
    stacked,
    masks,
    relu_f,
    shrink_f,
    weights,
    square,
    bias_row,
    modes,
    upstream,
    hidden,
    inner,
    grad_modes,
    leaving,
    returned,
    back_rows,
    own_sums,
    shared,
    result,
    result_out,
    east_v,
    north_v,
    turned_v,
    back_v,
    w_one_v,
    b_one_v,
    w_two_v,
    load_sem,
    self_sem,
    send_sem,
    recv_sem,
):
    nx, nz, ny = sizes
    devices = nx * nz * ny
    nlat = 2 * devices
    quarter = nlat // 4
    cx, cz, cy = (lax.axis_index(n) for n in NAMES)
    me = (cx * nz + cz) * ny + cy
    mine = lax.rem(me * pow(STEP, -1, devices), devices)

    def whom(x, z, y):
        return dict(zip(NAMES, (x, z, y)))

    def at_index(p):
        return whom(p // (nz * ny), lax.rem(p // ny, nz), lax.rem(p, ny))

    barrier = pltpu.get_barrier_semaphore()

    def greet(i, carry):
        d = at_index(lax.rem(me + i, devices))
        pl.semaphore_signal(barrier, inc=1, device_id=d, device_id_type=MESH)
        return carry

    loads = [
        pltpu.make_async_copy(src, dst, load_sem.at[i])
        for i, (src, dst) in enumerate(
            (
                (tok, raw.at[0]),
                (cot, raw.at[1]),
                (east_t, east_v),
                (relu, masks.at[0]),
                (shrink, masks.at[1]),
                (w_one, w_one_v),
                (b_one, b_one_v),
                (w_two, w_two_v),
                (north_t, north_v),
                (turned_t, turned_v),
                (back_t, back_v),
            )
        )
    ]
    for c in loads:
        c.start()
    lax.fori_loop(1, devices, greet, 0)

    lane = lane_of((ROWS, LANES))
    for i in range(4):
        spread[i, pl.ds(6 * GROUPS, 6 * (ROWS - GROUPS)), :] = jnp.zeros(
            (6 * (ROWS - GROUPS), LANES), F32
        )
    for f in range(2):
        loads[f].wait()
        for h in range(2):
            i = 2 * f + h
            spread[i, pl.ds(0, 6 * GROUPS), :] = raw[f, h].astype(F32)
            for j in range(4):
                b = [
                    block_of(
                        [spread[i, pl.ds(2 * c + n, ROWS, stride=6), :] for c in range(3)], j
                    )
                    for n in range(2)
                ]
                a0 = moved(b[0], FIRST[j], FIRST[0])
                a1 = moved(b[1], FIRST[j], FIRST[1])
                a2 = moved(b[0], FIRST[j], FIRST[2])
                a3 = moved(b[1], FIRST[j], FIRST[3])
                zero = jnp.zeros_like(a0)
                four = (
                    jnp.where(lane < 96, a0, a1),
                    jnp.where(lane < 64, a1, zero),
                    jnp.where(lane < 64, zero, a2),
                    jnp.where(lane < 32, a2, a3),
                )
                for t, v in enumerate(four):
                    packed[i, pl.ds(j * ROWS, ROWS), pl.ds(t * LANES, LANES)] = v.astype(BF16)
            if i == 0:
                loads[2].wait()
            for s in range(2):
                rows = pl.ds(s * devices, devices)
                even = dot(east_v[0, rows, :], packed[i, :, pl.ds(0, 256)])
                odd = dot(east_v[1, rows, :], packed[i, :, pl.ds(256, 256)])
                to = pl.ds(4 * f + 2 * s + h, devices, stride=8)
                wide[0, to, :] = even[:, :128]
                wide[1, to, :] = even[:, 128:] + odd[:, :128]
                wide[2, to, :] = odd[:, 128:]
    for c in range(3):
        ready[:, :, pl.ds(c * LANES, LANES)] = wide[c].reshape(devices, 8, LANES).astype(BF16)
    pl.semaphore_wait(barrier, devices - 1)

    def exchange(src, dst, n):
        def send(i, carry):
            p = lax.rem(me + i, devices)
            pltpu.make_async_remote_copy(
                src.at[pl.ds(p, 1)],
                dst.at[pl.ds(me, 1)],
                send_sem.at[n],
                recv_sem.at[n],
                device_id=at_index(p),
                device_id_type=MESH,
            ).start()
            return carry

        lax.fori_loop(1, devices, send, 0)
        own = pltpu.make_async_copy(src.at[pl.ds(me, 1)], dst.at[pl.ds(me, 1)], self_sem.at[n])
        own.start()
        many = pl.ds(0, devices - 1)
        whole = pltpu.make_async_remote_copy(
            src.at[many],
            dst.at[many],
            send_sem.at[n],
            recv_sem.at[n],
            device_id=whom(cx, lax.rem(cz + 1, nz), cy),
            device_id_type=MESH,
        )
        return own, whole

    own, whole = exchange(ready, arrived, 0)

    for c in loads[3:8]:
        c.wait()
    for m, to in ((0, relu_f), (1, shrink_f)):
        for s in range(2):
            for j in range(4):
                blocks = []
                for kn in range(4):
                    k, n = divmod(kn, 2)
                    three = [
                        masks[m, 2 * s + n, pl.ds(2 * c + k, quarter, stride=6), :]
                        for c in range(3)
                    ]
                    blocks.append(moved(block_of(three, j), FIRST[j], FIRST[kn]))
                for c, v in enumerate(tiles_of(blocks)):
                    to[pl.ds(s * nlat + j * quarter, quarter), pl.ds(c * LANES, LANES)] = v.astype(
                        F32
                    )
    square[...] = jnp.zeros_like(square)
    weights[...] = jnp.zeros_like(weights)
    column = lane_of((WIDTH, LANES))
    for m, src in ((0, w_one_v), (1, w_two_v)):
        for t in range(2):
            for n in range(2):
                square[:, pl.ds(0, WIDTH)] = src[t, n].astype(F32)
                base = square[...]
                for k in range(2):
                    kn = 2 * k + n
                    turned = moved(base, 0, FIRST[kn])
                    rows = pl.ds(kn * WIDTH, WIDTH)
                    if kn < 3:
                        keep = column >= FIRST[kn] if kn else column < WIDTH
                        c = (0, 0, 1)[kn]
                        weights[2 * m + t, rows, pl.ds(c * LANES, LANES)] = jnp.where(
                            keep, turned, 0.0
                        ).astype(BF16)
                    if kn > 0:
                        keep = column >= FIRST[3] if kn == 3 else column < FIRST[kn + 1]
                        c = (0, 1, 2, 2)[kn]
                        weights[2 * m + t, rows, pl.ds(c * LANES, LANES)] = jnp.where(
                            keep, turned, 0.0
                        ).astype(BF16)
    for t in range(2):
        for n in range(2):
            bias_row[pl.ds(2 * t + n, 1), pl.ds(0, WIDTH)] = b_one_v[t, pl.ds(n, 1), :].astype(F32)
    for t in range(2):
        blocks = [
            moved(
                jnp.broadcast_to(bias_row[pl.ds(2 * t + kn % 2, 1), pl.ds(0, LANES)], (8, LANES)),
                0,
                FIRST[kn],
            )
            for kn in range(4)
        ]
        for c, v in enumerate(tiles_of(blocks)):
            bias_row[pl.ds(8 + 8 * t, 8), pl.ds(c * LANES, LANES)] = v

    for c in loads[8:10]:
        c.wait()
    own.wait()
    whole.wait_recv()
    stacked[...] = arrived[...].reshape(8 * devices, 384)
    chunk = min(256, nlat)
    for f in (1, 0):
        for a in range(0, 2 * nlat, chunk):
            rows = pl.ds(a, chunk)
            value = dot(north_v[pl.ds(2 * f * nlat + a, chunk), :], stacked[...]).astype(BF16)
            if f:
                upstream[rows, :] = (value.astype(F32) * shrink_f[rows, :]).astype(BF16)
            else:
                modes[rows, :] = value

    half = min(128, nlat)
    parts = [(pl.ds(a, half), pl.ds(nlat + a, half)) for a in range(0, nlat, half)]

    def conjugate_mix(src, top, low, m):
        a, b = (src[top, :], src[low, :])
        real = dot_turned(a, weights[2 * m]) + dot_turned(b, weights[2 * m + 1])
        imag = dot_turned(b, weights[2 * m]) - dot_turned(a, weights[2 * m + 1])
        return real, imag

    for top, low in parts:
        real, imag = conjugate_mix(upstream, top, low, 1)
        inner[top, :] = (relu_f[top, :] * real).astype(BF16)
        inner[low, :] = (relu_f[low, :] * imag).astype(BF16)
    for top, low in parts:
        a, b = (modes[top, :], modes[low, :])
        real = dot(a, weights[0]) - dot(b, weights[1]) + bias_row[pl.ds(8, 1), :]
        imag = dot(a, weights[1]) + dot(b, weights[0]) + bias_row[pl.ds(16, 1), :]
        hidden[top, :] = (relu_f[top, :] * real).astype(BF16)
        hidden[low, :] = (relu_f[low, :] * imag).astype(BF16)
    upper, lower = (pl.ds(0, nlat), pl.ds(nlat, nlat))

    def diagonal(product, n, start):
        total = None
        for k in range(2):
            kn = 2 * k + n
            rows = product[kn * WIDTH : (kn + 1) * WIDTH]
            tiles = [rows[:, c * LANES : (c + 1) * LANES] for c in range(3)]
            block = moved(block_of(tiles, kn), FIRST[kn], start)
            total = block if total is None else total + block
        return total

    eighth = WIDTH // 8
    for g, (left, right) in enumerate(((modes, inner), (hidden, upstream))):
        real = dot_rows(left[...], right[...])
        imag = dot_rows(left[upper, :], right[lower, :]) - dot_rows(left[lower, :], right[upper, :])
        blocks = [
            diagonal(product, n, FIRST[2 * t + n])
            for t, product in enumerate((real, imag))
            for n in range(2)
        ]
        for c, v in enumerate(tiles_of(blocks)):
            shared[pl.ds((3 * g + c) * eighth, eighth)] = v.reshape(eighth, 8, LANES).astype(BF16)
    row8 = lax.broadcasted_iota(jnp.int32, (8, LANES), 0)
    total = jnp.zeros((8, LANES), F32)
    for t in range(2):
        sums = jnp.sum(inner[pl.ds(t * nlat, nlat), :].astype(F32), axis=0, keepdims=True)
        tiles = [
            jnp.broadcast_to(sums[:, c * LANES : (c + 1) * LANES], (8, LANES)) for c in range(3)
        ]
        for n in range(2):
            value = moved(block_of(tiles, n), FIRST[n], 0) + moved(
                block_of(tiles, 2 + n), FIRST[2 + n], 0
            )
            total = jnp.where(row8 == 2 * t + n, value, total)
    for spare in range(6 * eighth + 1, owners * per_owner):
        shared[spare] = jnp.zeros((8, LANES), BF16)
    shared[6 * eighth] = total.astype(BF16)

    def to_owner(i, carry):
        number = lax.rem(me + i, owners)
        p = lax.rem(number * STEP, devices)

        @pl.when(p != me)
        def _():
            pltpu.make_async_remote_copy(
                shared.at[pl.ds(number * per_owner, per_owner)],
                own_sums.at[me],
                send_sem.at[2],
                recv_sem.at[2],
                device_id=at_index(p),
                device_id_type=MESH,
            ).start()

        return carry

    lax.fori_loop(0, owners, to_owner, 0)
    whole.wait_send()

    for top, low in parts:
        real, imag = conjugate_mix(inner, top, low, 0)
        grad_modes[top, :] = real.astype(BF16)
        grad_modes[low, :] = imag.astype(BF16)
    for a in range(0, 4 * devices, half):
        value = dot(turned_v[pl.ds(a, half), :], grad_modes[...]).astype(BF16)
        leaving[pl.ds(a // 4, half // 4)] = value.reshape(half // 4, 4, 384)

    own_back, whole_back = exchange(leaving, returned, 1)

    neighbour = whom(cx, lax.rem(cz + 1, nz), cy)

    def bytes_of(ref, n):
        return pltpu.make_async_remote_copy(
            ref,
            ref,
            send_sem.at[n],
            recv_sem.at[n],
            device_id=neighbour,
            device_id_type=MESH,
        )

    @pl.when(mine < owners)
    def _():
        own_sums[me] = shared[pl.ds(mine * per_owner, per_owner)]
        bytes_of(own_sums.at[pl.ds(0, devices - 1)], 2).wait_recv()
        all_sums[mine] = jnp.sum(own_sums[...].astype(F32), axis=0).astype(BF16)

        def to_all(i, carry):
            pltpu.make_async_remote_copy(
                all_sums.at[mine],
                all_sums.at[mine],
                send_sem.at[3],
                recv_sem.at[3],
                device_id=at_index(lax.rem(me + i, devices)),
                device_id_type=MESH,
            ).start()
            return carry

        lax.fori_loop(1, devices, to_all, 0)

    stores = [pltpu.make_async_copy(raw.at[0, h], out.at[h], load_sem.at[h]) for h in range(2)]
    loads[10].wait()
    own_back.wait()
    whole_back.wait_recv()
    back_rows[...] = returned[...].reshape(4 * devices, 384)
    for h in range(2):
        for j in range(4):
            rows = pl.ds(j * ROWS, ROWS)
            even = dot(back_v[h, 0, rows, :], back_rows[:, pl.ds(0, 256)])
            odd = dot(back_v[h, 1, rows, :], back_rows[:, pl.ds(128, 256)])
            tiles = (even[:, :128], even[:, 128:], None)
            parted = (None, odd[:, :128], odd[:, 128:])
            for n in range(2):
                value = moved(block_of(tiles, n), FIRST[n], FIRST[j]) + moved(
                    block_of(parted, 2 + n), FIRST[2 + n], FIRST[j]
                ) if n == 1 else moved(tiles[0], FIRST[0], FIRST[j]) + moved(
                    jnp.where(lane >= FIRST[2], parted[1], parted[2]), FIRST[2], FIRST[j]
                )
                result_out[j, n] = value
        for n in range(2):
            for c, v in enumerate(tiles_of([result_out[j, n] for j in range(4)])):
                result[h, pl.ds(2 * c + n, ROWS, stride=6), :] = v
        done = result[h, pl.ds(0, 6 * GROUPS), :] + raw[1, h].astype(F32)
        raw[0, h] = done.astype(BF16)
        stores[h].start()

    whole_back.wait_send()

    @pl.when(mine < owners)
    def _():
        bytes_of(shared.at[pl.ds(0, (owners - 1) * per_owner)], 2).wait_send()
        bytes_of(own_sums.at[pl.ds(0, devices - 1)], 3).wait_send()
        bytes_of(all_sums.at[pl.ds(0, owners - 1)], 3).wait_recv()

    @pl.when(mine >= owners)
    def _():
        bytes_of(shared.at[pl.ds(0, owners * per_owner)], 2).wait_send()
        bytes_of(all_sums.at[pl.ds(0, owners)], 3).wait_recv()

    for c in stores:
        c.wait()


def finish(factor, ahead, sums, out, first_out, bias_out, second_out, sem):
    store = pltpu.make_async_copy(ahead, out, sem)
    store.start()
    eighth = WIDTH // 8
    for g, ref in enumerate((first_out, second_out)):
        tiles = [
            sums[pl.ds((3 * g + c) * eighth, eighth)].reshape(WIDTH, LANES).astype(F32)
            for c in range(3)
        ]
        for t in range(2):
            for n in range(2):
                i = 2 * t + n
                block = moved(block_of(tiles, i), FIRST[i], 0)
                ref[t, n] = block[:, :WIDTH] * factor
    last = sums[6 * eighth].astype(F32) * factor
    for t in range(2):
        bias_out[t] = last[2 * t : 2 * t + 2, :WIDTH]
    store.wait()


def local(sizes, tokens, cotangent, first_weight, first_bias, second_weight, relu_mask, shrink_mask):
    devices = math.prod(sizes)
    nlat = 2 * devices
    blocks = 6 * WIDTH // 8 + 1
    per_owner = max(2, -(-blocks // devices))
    owners = -(-blocks // per_owner)

    pairs = Layout(major_to_minor=(0, 2, 1, 3))

    def in_rows(field):
        tiles = with_layout_constraint(field.reshape(2, 2, 3 * GROUPS, LANES), pairs)
        return tiles.transpose(0, 2, 1, 3).reshape(2, 6 * GROUPS, LANES)

    def mask_rows(mask):
        width = mask.shape[-1] // LANES
        return (
            mask.reshape(4, 2, width, LANES).transpose(0, 2, 1, 3).reshape(4, 2 * width, LANES)
        )

    constants = [jnp.asarray(t) for t in tables(devices)]
    anywhere = pl.BlockSpec(memory_space=pl.ANY)
    in_vmem = pl.BlockSpec(memory_space=pltpu.VMEM)

    def vmem(*shape, dtype=BF16):
        return pltpu.VMEM(shape, dtype)

    ahead, sums = pl.pallas_call(
        functools.partial(kernel, sizes, per_owner, owners),
        out_shape=(
            jax.ShapeDtypeStruct((2, 6 * GROUPS, LANES), BF16),
            jax.ShapeDtypeStruct((owners, per_owner, 8, LANES), BF16),
        ),
        in_specs=[anywhere] * 11,
        out_specs=(anywhere, in_vmem),
        scratch_shapes=[
            vmem(2, 2, 6 * GROUPS, LANES),
            vmem(4, 6 * ROWS, LANES, dtype=F32),
            vmem(4, 4 * ROWS, 4 * LANES),
            vmem(3, 8 * devices, LANES, dtype=F32),
            vmem(devices, 8, 384),
            vmem(devices, 8, 384),
            vmem(8 * devices, 384),
            vmem(2, 4, 6 * (nlat // 4), LANES, dtype=jnp.int32),
            vmem(2 * nlat, 384, dtype=F32),
            vmem(2 * nlat, 384, dtype=F32),
            vmem(4, 384, 384),
            vmem(WIDTH, LANES, dtype=F32),
            vmem(24, 384, dtype=F32),
            vmem(2 * nlat, 384),
            vmem(2 * nlat, 384),
            vmem(2 * nlat, 384),
            vmem(2 * nlat, 384),
            vmem(2 * nlat, 384),
            vmem(devices, 4, 384),
            vmem(devices, 4, 384),
            vmem(4 * devices, 384),
            vmem(devices, per_owner, 8, LANES),
            vmem(owners * per_owner, 8, LANES),
            vmem(2, 6 * ROWS, LANES, dtype=F32),
            vmem(4, 2, ROWS, LANES, dtype=F32),
            vmem(*constants[0].shape),
            vmem(*constants[1].shape),
            vmem(*constants[2].shape),
            vmem(*constants[3].shape),
            vmem(*first_weight.shape),
            vmem(*first_bias.shape),
            vmem(*second_weight.shape),
            pltpu.SemaphoreType.DMA((11,)),
            pltpu.SemaphoreType.DMA((2,)),
            pltpu.SemaphoreType.DMA((4,)),
            pltpu.SemaphoreType.DMA((4,)),
        ],
        compiler_params=pltpu.CompilerParams(
            collective_id=0, has_side_effects=True, vmem_limit_bytes=60 * 1024 * 1024
        ),
    )(
        in_rows(tokens),
        in_rows(cotangent),
        first_weight,
        first_bias,
        second_weight,
        mask_rows(relu_mask),
        mask_rows(shrink_mask),
        *constants,
    )
    out, first, bias, second = pl.pallas_call(
        functools.partial(finish, 1.0 / math.sqrt(nlat * 2 * devices)),
        out_shape=(
            jax.ShapeDtypeStruct((2, 6 * GROUPS, LANES), BF16),
            jax.ShapeDtypeStruct(first_weight.shape, F32),
            jax.ShapeDtypeStruct(first_bias.shape, F32),
            jax.ShapeDtypeStruct(second_weight.shape, F32),
        ),
        in_specs=(anywhere, in_vmem),
        out_specs=(anywhere, in_vmem, in_vmem, in_vmem),
        scratch_shapes=[pltpu.SemaphoreType.DMA],
    )(ahead, sums.reshape(owners * per_owner, 8, LANES))
    out = out.reshape(2, 3 * GROUPS, 2, LANES).transpose(0, 2, 1, 3)
    token_gradient = with_layout_constraint(out, pairs).reshape(tokens.shape)
    return (token_gradient, first, bias, second)


def solution(mesh, sizes=(4, 8, 4)):
    finer = Mesh(mesh.devices.reshape(*sizes, mesh.shape["ch"]), (*NAMES, "ch"))
    in_specs = (
        P(None, NAMES, "ch", None),
        P(None, NAMES, "ch", None),
        P(None, "ch", None, None),
        P(None, "ch", None),
        P(None, "ch", None, None),
        P(None, None, "ch", NAMES, None),
        P(None, None, "ch", NAMES, None),
    )
    out_specs = (
        P(None, NAMES, "ch", None),
        P(None, "ch", None, None),
        P(None, "ch", None),
        P(None, "ch", None, None),
    )
    return jax.shard_map(
        functools.partial(local, sizes),
        mesh=finer,
        in_specs=in_specs,
        out_specs=out_specs,
        check_vma=False,
    )
```

```python
import functools
import math

import jax
import jax.numpy as jnp
import ml_dtypes
import numpy as np
from jax import lax
from jax.experimental import pallas as pl
from jax.experimental.layout import Layout, with_layout_constraint
from jax.experimental.pallas import tpu as pltpu
from jax.sharding import Mesh
from jax.sharding import PartitionSpec as P

MESH = pl.DeviceIdType.MESH
NAMES = ("lat_0", "lat_1", "lat_2")
WIDTH = 96
LANES = 128
ROWS = 192
GROUPS = 180
F32 = jnp.float32
BF16 = jnp.bfloat16
FIRST = (0, 96, 64, 32)


def tables(devices):
    nlat, nlon = (2 * devices, 4 * GROUPS)
    w = np.arange(nlon)[:, None]
    k = np.arange(2 * devices)[None, :]
    phase = (w * k % nlon) * (2.0 * math.pi / nlon)
    east = np.stack([np.cos(phase), -np.sin(phase)], axis=1) / math.sqrt(nlon)
    east = east.reshape(GROUPS, 4, 2, devices, 2).transpose(1, 0, 2, 3, 4)
    filled = np.zeros((4, ROWS, 2, devices, 2))
    filled[:, :GROUPS] = east
    out_east = filled.transpose(4, 2, 3, 0, 1).reshape(2, 2 * devices, 4 * ROWS)
    back = np.zeros((2, 2, 4, ROWS, devices, 2, 2))
    for h in range(2):
        back[h, :, :, :, :, :, h] = filled.transpose(4, 0, 1, 3, 2)
    back = back.reshape(2, 2, 4 * ROWS, 4 * devices)
    q = np.arange(nlat)[:, None]
    h = np.arange(nlat)[None, :]
    phase = (q * h % nlat) * (2.0 * math.pi / nlat)
    cosine, sine = (np.cos(phase) / math.sqrt(nlat), np.sin(phase) / math.sqrt(nlat))
    north = np.stack([np.stack([cosine, sine]), np.stack([-sine, cosine])])
    north = north.transpose(0, 2, 1, 3).reshape(2, nlat // 4, 4, 2, devices, 2)
    north = north.transpose(0, 2, 1, 4, 3, 5).reshape(2 * nlat, devices, 4)
    both = np.zeros((2, 2 * nlat, devices, 2, 4))
    for f in range(2):
        both[f, :, :, f] = north
    both = both.reshape(4 * nlat, 8 * devices)
    turned = north.reshape(2 * nlat, 4 * devices).T
    return tuple(
        np.ascontiguousarray(t.astype(np.float32).astype(ml_dtypes.bfloat16))
        for t in (out_east, both, turned, back)
    )


def lane_of(shape):
    return lax.broadcasted_iota(jnp.int32, shape, 1)


def moved(block, start, end):
    shift = (end - start) % LANES
    return block if shift == 0 else pltpu.roll(block, shift, 1)


def block_of(tiles, i):
    if i == 0:
        return tiles[0]
    if i == 3:
        return tiles[2]
    lane = lane_of(tiles[0].shape)
    return jnp.where(lane >= FIRST[i], tiles[i - 1], tiles[i])


def tiles_of(blocks):
    lane = lane_of(blocks[0].shape)
    return [jnp.where(lane < FIRST[i + 1], blocks[i], blocks[i + 1]) for i in range(3)]


def dot(a, b):
    return lax.dot_general(a, b, (((1,), (0,)), ((), ())), preferred_element_type=F32)


def dot_rows(a, b):
    return lax.dot_general(a, b, (((0,), (0,)), ((), ())), preferred_element_type=F32)


def dot_turned(a, b):
    return lax.dot_general(a, b, (((1,), (1,)), ((), ())), preferred_element_type=F32)


def kernel(
    sizes,
    per_owner,
    owners,
    tok,
    cot,
    w_one,
    b_one,
    w_two,
    relu,
    shrink,
    east_t,
    north_t,
    turned_t,
    back_t,
    out,
    all_sums,
    raw,
    spread,
    packed,
    wide,
    ready,
    arrived,
    stacked,
    masks,
    relu_f,
    shrink_f,
    weights,
    square,
    bias_row,
    modes,
    upstream,
    hidden,
    inner,
    grad_modes,
    leaving,
    returned,
    back_rows,
    own_sums,
    shared,
    result,
    result_out,
    east_v,
    north_v,
    turned_v,
    back_v,
    w_one_v,
    b_one_v,
    w_two_v,
    load_sem,
    self_sem,
    send_sem,
    recv_sem,
):
    nx, nz, ny = sizes
    devices = nx * nz * ny
    nlat = 2 * devices
    quarter = nlat // 4
    cx, cz, cy = (lax.axis_index(n) for n in NAMES)
    me = (cx * nz + cz) * ny + cy

    def whom(x, z, y):
        return dict(zip(NAMES, (x, z, y)))

    def at_index(p):
        return whom(p // (nz * ny), lax.rem(p // ny, nz), lax.rem(p, ny))

    barrier = pltpu.get_barrier_semaphore()

    def greet(i, carry):
        step, j = (i // (nx * ny), lax.rem(i, nx * ny))
        far = (step + 1) // 2 * (1 - 2 * lax.rem(step, 2))
        z = lax.rem(cz + nz + nz // 2 + far, nz)
        x = lax.rem(cx + nx // 2 + j // ny, nx)
        y = lax.rem(cy + ny // 2 + lax.rem(j, ny), ny)

        @pl.when(i != devices - nx * ny + nx // 2 * ny + ny // 2)
        def _():
            pl.semaphore_signal(barrier, inc=1, device_id=whom(x, z, y), device_id_type=MESH)

        return carry

    loads = [
        pltpu.make_async_copy(src, dst, load_sem.at[i])
        for i, (src, dst) in enumerate(
            (
                (tok, raw.at[0]),
                (cot, raw.at[1]),
                (east_t, east_v),
                (relu, masks.at[0]),
                (shrink, masks.at[1]),
                (w_one, w_one_v),
                (b_one, b_one_v),
                (w_two, w_two_v),
                (north_t, north_v),
                (turned_t, turned_v),
                (back_t, back_v),
            )
        )
    ]
    for c in loads[:3]:
        c.start()
    lax.fori_loop(0, devices, greet, 0)
    for c in loads[3:]:
        c.start()

    lane = lane_of((ROWS, LANES))
    for i in range(4):
        spread[i, pl.ds(6 * GROUPS, 6 * (ROWS - GROUPS)), :] = jnp.zeros(
            (6 * (ROWS - GROUPS), LANES), F32
        )
    for f in range(2):
        loads[f].wait()
        for h in range(2):
            i = 2 * f + h
            spread[i, pl.ds(0, 6 * GROUPS), :] = raw[f, h].astype(F32)
            for j in range(4):
                b = [
                    block_of(
                        [spread[i, pl.ds(2 * c + n, ROWS, stride=6), :] for c in range(3)], j
                    )
                    for n in range(2)
                ]
                a0 = moved(b[0], FIRST[j], FIRST[0])
                a1 = moved(b[1], FIRST[j], FIRST[1])
                a2 = moved(b[0], FIRST[j], FIRST[2])
                a3 = moved(b[1], FIRST[j], FIRST[3])
                zero = jnp.zeros_like(a0)
                four = (
                    jnp.where(lane < 96, a0, a1),
                    jnp.where(lane < 64, a1, zero),
                    jnp.where(lane < 64, zero, a2),
                    jnp.where(lane < 32, a2, a3),
                )
                for t, v in enumerate(four):
                    packed[i, pl.ds(j * ROWS, ROWS), pl.ds(t * LANES, LANES)] = v.astype(BF16)
            if i == 0:
                loads[2].wait()
            for s in range(2):
                rows = pl.ds(s * devices, devices)
                even = dot(east_v[0, rows, :], packed[i, :, pl.ds(0, 256)])
                odd = dot(east_v[1, rows, :], packed[i, :, pl.ds(256, 256)])
                to = pl.ds(4 * f + 2 * s + h, devices, stride=8)
                wide[0, to, :] = even[:, :128]
                wide[1, to, :] = even[:, 128:] + odd[:, :128]
                wide[2, to, :] = odd[:, 128:]
    for c in range(3):
        ready[:, :, pl.ds(c * LANES, LANES)] = wide[c].reshape(devices, 8, LANES).astype(BF16)
    pl.semaphore_wait(barrier, devices - 1)

    def exchange(src, dst, n):
        def send(i, carry):
            p = lax.rem(me + i, devices)
            pltpu.make_async_remote_copy(
                src.at[pl.ds(p, 1)],
                dst.at[pl.ds(me, 1)],
                send_sem.at[n],
                recv_sem.at[n],
                device_id=at_index(p),
                device_id_type=MESH,
            ).start()
            return carry

        lax.fori_loop(1, devices, send, 0)
        own = pltpu.make_async_copy(src.at[pl.ds(me, 1)], dst.at[pl.ds(me, 1)], self_sem.at[n])
        own.start()
        many = pl.ds(0, devices - 1)
        whole = pltpu.make_async_remote_copy(
            src.at[many],
            dst.at[many],
            send_sem.at[n],
            recv_sem.at[n],
            device_id=whom(cx, lax.rem(cz + 1, nz), cy),
            device_id_type=MESH,
        )
        return own, whole

    own, whole = exchange(ready, arrived, 0)

    for c in loads[3:8]:
        c.wait()
    for m, to in ((0, relu_f), (1, shrink_f)):
        for s in range(2):
            for j in range(4):
                blocks = []
                for kn in range(4):
                    k, n = divmod(kn, 2)
                    three = [
                        masks[m, 2 * s + n, pl.ds(2 * c + k, quarter, stride=6), :]
                        for c in range(3)
                    ]
                    blocks.append(moved(block_of(three, j), FIRST[j], FIRST[kn]))
                for c, v in enumerate(tiles_of(blocks)):
                    to[pl.ds(s * nlat + j * quarter, quarter), pl.ds(c * LANES, LANES)] = v.astype(
                        F32
                    )
    square[...] = jnp.zeros_like(square)
    weights[...] = jnp.zeros_like(weights)
    column = lane_of((WIDTH, LANES))
    for m, src in ((0, w_one_v), (1, w_two_v)):
        for t in range(2):
            for n in range(2):
                square[:, pl.ds(0, WIDTH)] = src[t, n].astype(F32)
                base = square[...]
                for k in range(2):
                    kn = 2 * k + n
                    turned = moved(base, 0, FIRST[kn])
                    rows = pl.ds(kn * WIDTH, WIDTH)
                    if kn < 3:
                        keep = column >= FIRST[kn] if kn else column < WIDTH
                        c = (0, 0, 1)[kn]
                        weights[2 * m + t, rows, pl.ds(c * LANES, LANES)] = jnp.where(
                            keep, turned, 0.0
                        ).astype(BF16)
                    if kn > 0:
                        keep = column >= FIRST[3] if kn == 3 else column < FIRST[kn + 1]
                        c = (0, 1, 2, 2)[kn]
                        weights[2 * m + t, rows, pl.ds(c * LANES, LANES)] = jnp.where(
                            keep, turned, 0.0
                        ).astype(BF16)
    for t in range(2):
        for n in range(2):
            bias_row[pl.ds(2 * t + n, 1), pl.ds(0, WIDTH)] = b_one_v[t, pl.ds(n, 1), :].astype(F32)
    for t in range(2):
        blocks = [
            moved(
                jnp.broadcast_to(bias_row[pl.ds(2 * t + kn % 2, 1), pl.ds(0, LANES)], (8, LANES)),
                0,
                FIRST[kn],
            )
            for kn in range(4)
        ]
        for c, v in enumerate(tiles_of(blocks)):
            bias_row[pl.ds(8 + 8 * t, 8), pl.ds(c * LANES, LANES)] = v

    for c in loads[8:10]:
        c.wait()
    own.wait()
    whole.wait_recv()
    stacked[...] = arrived[...].reshape(8 * devices, 384)
    chunk = min(256, nlat)
    for f in (1, 0):
        for a in range(0, 2 * nlat, chunk):
            rows = pl.ds(a, chunk)
            value = dot(north_v[pl.ds(2 * f * nlat + a, chunk), :], stacked[...]).astype(BF16)
            if f:
                upstream[rows, :] = (value.astype(F32) * shrink_f[rows, :]).astype(BF16)
            else:
                modes[rows, :] = value

    half = min(128, nlat)
    parts = [(pl.ds(a, half), pl.ds(nlat + a, half)) for a in range(0, nlat, half)]

    def conjugate_mix(src, top, low, m):
        a, b = (src[top, :], src[low, :])
        real = dot_turned(a, weights[2 * m]) + dot_turned(b, weights[2 * m + 1])
        imag = dot_turned(b, weights[2 * m]) - dot_turned(a, weights[2 * m + 1])
        return real, imag

    for top, low in parts:
        real, imag = conjugate_mix(upstream, top, low, 1)
        inner[top, :] = (relu_f[top, :] * real).astype(BF16)
        inner[low, :] = (relu_f[low, :] * imag).astype(BF16)
    for top, low in parts:
        a, b = (modes[top, :], modes[low, :])
        real = dot(a, weights[0]) - dot(b, weights[1]) + bias_row[pl.ds(8, 1), :]
        imag = dot(a, weights[1]) + dot(b, weights[0]) + bias_row[pl.ds(16, 1), :]
        hidden[top, :] = (relu_f[top, :] * real).astype(BF16)
        hidden[low, :] = (relu_f[low, :] * imag).astype(BF16)
    upper, lower = (pl.ds(0, nlat), pl.ds(nlat, nlat))

    def diagonal(product, n, start):
        total = None
        for k in range(2):
            kn = 2 * k + n
            rows = product[kn * WIDTH : (kn + 1) * WIDTH]
            tiles = [rows[:, c * LANES : (c + 1) * LANES] for c in range(3)]
            block = moved(block_of(tiles, kn), FIRST[kn], start)
            total = block if total is None else total + block
        return total

    eighth = WIDTH // 8
    for g, (left, right) in enumerate(((modes, inner), (hidden, upstream))):
        real = dot_rows(left[...], right[...])
        imag = dot_rows(left[upper, :], right[lower, :]) - dot_rows(left[lower, :], right[upper, :])
        blocks = [
            diagonal(product, n, FIRST[2 * t + n])
            for t, product in enumerate((real, imag))
            for n in range(2)
        ]
        for c, v in enumerate(tiles_of(blocks)):
            shared[pl.ds((3 * g + c) * eighth, eighth)] = v.reshape(eighth, 8, LANES).astype(BF16)
    row8 = lax.broadcasted_iota(jnp.int32, (8, LANES), 0)
    total = jnp.zeros((8, LANES), F32)
    for t in range(2):
        sums = jnp.sum(inner[pl.ds(t * nlat, nlat), :].astype(F32), axis=0, keepdims=True)
        tiles = [
            jnp.broadcast_to(sums[:, c * LANES : (c + 1) * LANES], (8, LANES)) for c in range(3)
        ]
        for n in range(2):
            value = moved(block_of(tiles, n), FIRST[n], 0) + moved(
                block_of(tiles, 2 + n), FIRST[2 + n], 0
            )
            total = jnp.where(row8 == 2 * t + n, value, total)
    shared[6 * eighth] = total.astype(BF16)

    def to_owner(i, carry):
        p = lax.rem(me + i, owners)

        @pl.when(p != me)
        def _():
            pltpu.make_async_remote_copy(
                shared.at[pl.ds(p * per_owner, per_owner)],
                own_sums.at[me],
                send_sem.at[2],
                recv_sem.at[2],
                device_id=at_index(p),
                device_id_type=MESH,
            ).start()

        return carry

    lax.fori_loop(0, owners, to_owner, 0)
    whole.wait_send()

    for top, low in parts:
        real, imag = conjugate_mix(inner, top, low, 0)
        grad_modes[top, :] = real.astype(BF16)
        grad_modes[low, :] = imag.astype(BF16)
    for a in range(0, 4 * devices, half):
        value = dot(turned_v[pl.ds(a, half), :], grad_modes[...]).astype(BF16)
        leaving[pl.ds(a // 4, half // 4)] = value.reshape(half // 4, 4, 384)

    own_back, whole_back = exchange(leaving, returned, 1)

    neighbour = whom(cx, lax.rem(cz + 1, nz), cy)

    def bytes_of(ref, n):
        return pltpu.make_async_remote_copy(
            ref,
            ref,
            send_sem.at[n],
            recv_sem.at[n],
            device_id=neighbour,
            device_id_type=MESH,
        )

    @pl.when(me < owners)
    def _():
        own_sums[me] = shared[pl.ds(me * per_owner, per_owner)]
        bytes_of(own_sums.at[pl.ds(0, devices - 1)], 2).wait_recv()
        all_sums[me] = jnp.sum(own_sums[...].astype(F32), axis=0).astype(BF16)

        def to_all(i, carry):
            pltpu.make_async_remote_copy(
                all_sums.at[me],
                all_sums.at[me],
                send_sem.at[3],
                recv_sem.at[3],
                device_id=at_index(lax.rem(me + i, devices)),
                device_id_type=MESH,
            ).start()
            return carry

        lax.fori_loop(1, devices, to_all, 0)

    stores = [pltpu.make_async_copy(raw.at[0, h], out.at[h], load_sem.at[h]) for h in range(2)]
    loads[10].wait()
    own_back.wait()
    whole_back.wait_recv()
    back_rows[...] = returned[...].reshape(4 * devices, 384)
    for h in range(2):
        for j in range(4):
            rows = pl.ds(j * ROWS, ROWS)
            even = dot(back_v[h, 0, rows, :], back_rows[:, pl.ds(0, 256)])
            odd = dot(back_v[h, 1, rows, :], back_rows[:, pl.ds(128, 256)])
            tiles = (even[:, :128], even[:, 128:], None)
            parted = (None, odd[:, :128], odd[:, 128:])
            for n in range(2):
                value = moved(block_of(tiles, n), FIRST[n], FIRST[j]) + moved(
                    block_of(parted, 2 + n), FIRST[2 + n], FIRST[j]
                ) if n == 1 else moved(tiles[0], FIRST[0], FIRST[j]) + moved(
                    jnp.where(lane >= FIRST[2], parted[1], parted[2]), FIRST[2], FIRST[j]
                )
                result_out[j, n] = value
        for n in range(2):
            for c, v in enumerate(tiles_of([result_out[j, n] for j in range(4)])):
                result[h, pl.ds(2 * c + n, ROWS, stride=6), :] = v
        done = result[h, pl.ds(0, 6 * GROUPS), :] + raw[1, h].astype(F32)
        raw[0, h] = done.astype(BF16)
        stores[h].start()

    whole_back.wait_send()

    @pl.when(me < owners)
    def _():
        bytes_of(shared.at[pl.ds(0, (owners - 1) * per_owner)], 2).wait_send()
        bytes_of(own_sums.at[pl.ds(0, devices - 1)], 3).wait_send()
        bytes_of(all_sums.at[pl.ds(0, owners - 1)], 3).wait_recv()

    @pl.when(me >= owners)
    def _():
        bytes_of(shared.at[pl.ds(0, owners * per_owner)], 2).wait_send()
        bytes_of(all_sums.at[pl.ds(0, owners)], 3).wait_recv()

    for c in stores:
        c.wait()


def finish(factor, ahead, sums, out, first_out, bias_out, second_out, held, in_sem, out_sem):
    fetch = [pltpu.make_async_copy(ahead.at[h], held.at[h], in_sem.at[h]) for h in range(2)]
    store = [pltpu.make_async_copy(held.at[h], out.at[h], out_sem.at[h]) for h in range(2)]
    for c in fetch:
        c.start()
    for h in range(2):
        fetch[h].wait()
        store[h].start()
    eighth = WIDTH // 8
    for g, ref in enumerate((first_out, second_out)):
        tiles = [
            sums[pl.ds((3 * g + c) * eighth, eighth)].reshape(WIDTH, LANES).astype(F32)
            for c in range(3)
        ]
        for t in range(2):
            for n in range(2):
                i = 2 * t + n
                block = moved(block_of(tiles, i), FIRST[i], 0)
                ref[t, n] = block[:, :WIDTH] * factor
    last = sums[6 * eighth].astype(F32) * factor
    for t in range(2):
        bias_out[t] = last[2 * t : 2 * t + 2, :WIDTH]
    for c in store:
        c.wait()


def local(sizes, tokens, cotangent, first_weight, first_bias, second_weight, relu_mask, shrink_mask):
    devices = math.prod(sizes)
    nlat = 2 * devices
    blocks = 6 * WIDTH // 8 + 1
    per_owner = -(-blocks // devices)
    owners = -(-blocks // per_owner)

    pairs = Layout(major_to_minor=(0, 2, 1, 3))

    def in_rows(field):
        tiles = with_layout_constraint(field.reshape(2, 2, 3 * GROUPS, LANES), pairs)
        return tiles.transpose(0, 2, 1, 3).reshape(2, 6 * GROUPS, LANES)

    def mask_rows(mask):
        width = mask.shape[-1] // LANES
        return (
            mask.reshape(4, 2, width, LANES).transpose(0, 2, 1, 3).reshape(4, 2 * width, LANES)
        )

    constants = [jnp.asarray(t) for t in tables(devices)]
    anywhere = pl.BlockSpec(memory_space=pl.ANY)
    in_vmem = pl.BlockSpec(memory_space=pltpu.VMEM)

    def vmem(*shape, dtype=BF16):
        return pltpu.VMEM(shape, dtype)

    ahead, sums = pl.pallas_call(
        functools.partial(kernel, sizes, per_owner, owners),
        out_shape=(
            jax.ShapeDtypeStruct((2, 6 * GROUPS, LANES), BF16),
            jax.ShapeDtypeStruct((owners, per_owner, 8, LANES), BF16),
        ),
        in_specs=[anywhere] * 11,
        out_specs=(anywhere, in_vmem),
        scratch_shapes=[
            vmem(2, 2, 6 * GROUPS, LANES),
            vmem(4, 6 * ROWS, LANES, dtype=F32),
            vmem(4, 4 * ROWS, 4 * LANES),
            vmem(3, 8 * devices, LANES, dtype=F32),
            vmem(devices, 8, 384),
            vmem(devices, 8, 384),
            vmem(8 * devices, 384),
            vmem(2, 4, 6 * (nlat // 4), LANES, dtype=jnp.int32),
            vmem(2 * nlat, 384, dtype=F32),
            vmem(2 * nlat, 384, dtype=F32),
            vmem(4, 384, 384),
            vmem(WIDTH, LANES, dtype=F32),
            vmem(24, 384, dtype=F32),
            vmem(2 * nlat, 384),
            vmem(2 * nlat, 384),
            vmem(2 * nlat, 384),
            vmem(2 * nlat, 384),
            vmem(2 * nlat, 384),
            vmem(devices, 4, 384),
            vmem(devices, 4, 384),
            vmem(4 * devices, 384),
            vmem(devices, per_owner, 8, LANES),
            vmem(owners * per_owner, 8, LANES),
            vmem(2, 6 * ROWS, LANES, dtype=F32),
            vmem(4, 2, ROWS, LANES, dtype=F32),
            vmem(*constants[0].shape),
            vmem(*constants[1].shape),
            vmem(*constants[2].shape),
            vmem(*constants[3].shape),
            vmem(*first_weight.shape),
            vmem(*first_bias.shape),
            vmem(*second_weight.shape),
            pltpu.SemaphoreType.DMA((11,)),
            pltpu.SemaphoreType.DMA((2,)),
            pltpu.SemaphoreType.DMA((4,)),
            pltpu.SemaphoreType.DMA((4,)),
        ],
        compiler_params=pltpu.CompilerParams(
            collective_id=0, has_side_effects=True, vmem_limit_bytes=60 * 1024 * 1024
        ),
    )(
        in_rows(tokens),
        in_rows(cotangent),
        first_weight,
        first_bias,
        second_weight,
        mask_rows(relu_mask),
        mask_rows(shrink_mask),
        *constants,
    )
    out, first, bias, second = pl.pallas_call(
        functools.partial(finish, 1.0 / math.sqrt(nlat * 2 * devices)),
        out_shape=(
            jax.ShapeDtypeStruct((2, 6 * GROUPS, LANES), BF16),
            jax.ShapeDtypeStruct(first_weight.shape, F32),
            jax.ShapeDtypeStruct(first_bias.shape, F32),
            jax.ShapeDtypeStruct(second_weight.shape, F32),
        ),
        in_specs=(anywhere, in_vmem),
        out_specs=(anywhere, in_vmem, in_vmem, in_vmem),
        scratch_shapes=[
            vmem(2, 6 * GROUPS, LANES),
            pltpu.SemaphoreType.DMA((2,)),
            pltpu.SemaphoreType.DMA((2,)),
        ],
    )(ahead, sums.reshape(owners * per_owner, 8, LANES))
    out = out.reshape(2, 3 * GROUPS, 2, LANES).transpose(0, 2, 1, 3)
    token_gradient = with_layout_constraint(out, pairs).reshape(tokens.shape)
    return (token_gradient, first, bias, second)


def solution(mesh, sizes=(4, 8, 4)):
    finer = Mesh(mesh.devices.reshape(*sizes, mesh.shape["ch"]), (*NAMES, "ch"))
    in_specs = (
        P(None, NAMES, "ch", None),
        P(None, NAMES, "ch", None),
        P(None, "ch", None, None),
        P(None, "ch", None),
        P(None, "ch", None, None),
        P(None, None, "ch", NAMES, None),
        P(None, None, "ch", NAMES, None),
    )
    out_specs = (
        P(None, NAMES, "ch", None),
        P(None, "ch", None, None),
        P(None, "ch", None),
        P(None, "ch", None, None),
    )
    return jax.shard_map(
        functools.partial(local, sizes),
        mesh=finer,
        in_specs=in_specs,
        out_specs=out_specs,
        check_vma=False,
    )
```

```python
import functools
import math

import jax
import jax.numpy as jnp
import ml_dtypes
import numpy as np
from jax import lax
from jax.experimental import pallas as pl
from jax.experimental.layout import Layout, with_layout_constraint
from jax.experimental.pallas import tpu as pltpu
from jax.sharding import Mesh
from jax.sharding import PartitionSpec as P

MESH = pl.DeviceIdType.MESH
NAMES = ("lat_0", "lat_1", "lat_2")
WIDTH = 96
LANES = 128
ROWS = 192
GROUPS = 180
F32 = jnp.float32
BF16 = jnp.bfloat16
FIRST = (0, 96, 64, 32)


def tables(devices):
    nlat, nlon = (2 * devices, 4 * GROUPS)
    w = np.arange(nlon)[:, None]
    k = np.arange(2 * devices)[None, :]
    phase = (w * k % nlon) * (2.0 * math.pi / nlon)
    east = np.stack([np.cos(phase), -np.sin(phase)], axis=1) / math.sqrt(nlon)
    east = east.reshape(GROUPS, 4, 2, devices, 2).transpose(1, 0, 2, 3, 4)
    filled = np.zeros((4, ROWS, 2, devices, 2))
    filled[:, :GROUPS] = east
    out_east = filled.transpose(4, 2, 3, 0, 1).reshape(2, 2 * devices, 4 * ROWS)
    back = np.zeros((2, 2, 4, ROWS, devices, 2, 2))
    for h in range(2):
        back[h, :, :, :, :, :, h] = filled.transpose(4, 0, 1, 3, 2)
    back = back.reshape(2, 2, 4 * ROWS, 4 * devices)
    q = np.arange(nlat)[:, None]
    h = np.arange(nlat)[None, :]
    phase = (q * h % nlat) * (2.0 * math.pi / nlat)
    cosine, sine = (np.cos(phase) / math.sqrt(nlat), np.sin(phase) / math.sqrt(nlat))
    north = np.stack([np.stack([cosine, sine]), np.stack([-sine, cosine])])
    north = north.transpose(0, 2, 1, 3).reshape(2, nlat // 4, 4, 2, devices, 2)
    north = north.transpose(0, 2, 1, 4, 3, 5).reshape(2 * nlat, devices, 4)
    both = np.zeros((2, 2 * nlat, devices, 2, 4))
    for f in range(2):
        both[f, :, :, f] = north
    both = both.reshape(4 * nlat, 8 * devices)
    turned = north.reshape(2 * nlat, 4 * devices).T
    return tuple(
        np.ascontiguousarray(t.astype(np.float32).astype(ml_dtypes.bfloat16))
        for t in (out_east, both, turned, back)
    )


def lane_of(shape):
    return lax.broadcasted_iota(jnp.int32, shape, 1)


def moved(block, start, end):
    shift = (end - start) % LANES
    return block if shift == 0 else pltpu.roll(block, shift, 1)


def block_of(tiles, i):
    if i == 0:
        return tiles[0]
    if i == 3:
        return tiles[2]
    lane = lane_of(tiles[0].shape)
    return jnp.where(lane >= FIRST[i], tiles[i - 1], tiles[i])


def tiles_of(blocks):
    lane = lane_of(blocks[0].shape)
    return [jnp.where(lane < FIRST[i + 1], blocks[i], blocks[i + 1]) for i in range(3)]


def dot(a, b):
    return lax.dot_general(a, b, (((1,), (0,)), ((), ())), preferred_element_type=F32)


def dot_rows(a, b):
    return lax.dot_general(a, b, (((0,), (0,)), ((), ())), preferred_element_type=F32)


def dot_turned(a, b):
    return lax.dot_general(a, b, (((1,), (1,)), ((), ())), preferred_element_type=F32)


def kernel(
    sizes,
    per_owner,
    owners,
    tok,
    cot,
    w_one,
    b_one,
    w_two,
    relu,
    shrink,
    east_t,
    north_t,
    turned_t,
    back_t,
    out,
    all_sums,
    raw,
    spread,
    packed,
    wide,
    ready,
    arrived,
    stacked,
    masks,
    relu_f,
    shrink_f,
    weights,
    square,
    bias_row,
    modes,
    upstream,
    hidden,
    inner,
    grad_modes,
    leaving,
    returned,
    back_rows,
    own_sums,
    shared,
    result,
    result_out,
    east_v,
    north_v,
    turned_v,
    back_v,
    w_one_v,
    b_one_v,
    w_two_v,
    load_sem,
    self_sem,
    send_sem,
    recv_sem,
):
    nx, nz, ny = sizes
    devices = nx * nz * ny
    assert all(n & (n - 1) == 0 for n in sizes)
    nlat = 2 * devices
    quarter = nlat // 4
    cx, cz, cy = (lax.axis_index(n) for n in NAMES)
    me = (cx * nz + cz) * ny + cy

    def whom(x, z, y):
        return dict(zip(NAMES, (x, z, y)))

    def at_index(p):
        zy = lax.shift_right_logical(p, ny.bit_length() - 1)
        x = lax.shift_right_logical(zy, nz.bit_length() - 1)
        return whom(x, lax.bitwise_and(zy, nz - 1), lax.bitwise_and(p, ny - 1))

    barrier = pltpu.get_barrier_semaphore()

    def greet(i, carry):
        d = at_index(lax.bitwise_and(me + i, devices - 1))
        pl.semaphore_signal(barrier, inc=1, device_id=d, device_id_type=MESH)
        return carry

    loads = [
        pltpu.make_async_copy(src, dst, load_sem.at[i])
        for i, (src, dst) in enumerate(
            (
                (tok, raw.at[0]),
                (cot, raw.at[1]),
                (east_t, east_v),
                (relu, masks.at[0]),
                (shrink, masks.at[1]),
                (w_one, w_one_v),
                (b_one, b_one_v),
                (w_two, w_two_v),
                (north_t, north_v),
                (turned_t, turned_v),
                (back_t, back_v),
            )
        )
    ]
    for c in loads:
        c.start()
    lax.fori_loop(1, devices, greet, 0)

    lane = lane_of((ROWS, LANES))
    for i in range(4):
        spread[i, pl.ds(6 * GROUPS, 6 * (ROWS - GROUPS)), :] = jnp.zeros(
            (6 * (ROWS - GROUPS), LANES), F32
        )
    for f in range(2):
        loads[f].wait()
        for h in range(2):
            i = 2 * f + h
            spread[i, pl.ds(0, 6 * GROUPS), :] = raw[f, h].astype(F32)
            for j in range(4):
                b = [
                    block_of(
                        [spread[i, pl.ds(2 * c + n, ROWS, stride=6), :] for c in range(3)], j
                    )
                    for n in range(2)
                ]
                a0 = moved(b[0], FIRST[j], FIRST[0])
                a1 = moved(b[1], FIRST[j], FIRST[1])
                a2 = moved(b[0], FIRST[j], FIRST[2])
                a3 = moved(b[1], FIRST[j], FIRST[3])
                zero = jnp.zeros_like(a0)
                four = (
                    jnp.where(lane < 96, a0, a1),
                    jnp.where(lane < 64, a1, zero),
                    jnp.where(lane < 64, zero, a2),
                    jnp.where(lane < 32, a2, a3),
                )
                for t, v in enumerate(four):
                    packed[i, pl.ds(j * ROWS, ROWS), pl.ds(t * LANES, LANES)] = v.astype(BF16)
            if i == 0:
                loads[2].wait()
            for s in range(2):
                rows = pl.ds(s * devices, devices)
                even = dot(east_v[0, rows, :], packed[i, :, pl.ds(0, 256)])
                odd = dot(east_v[1, rows, :], packed[i, :, pl.ds(256, 256)])
                to = pl.ds(4 * f + 2 * s + h, devices, stride=8)
                wide[0, to, :] = even[:, :128]
                wide[1, to, :] = even[:, 128:] + odd[:, :128]
                wide[2, to, :] = odd[:, 128:]
    for c in range(3):
        ready[:, :, pl.ds(c * LANES, LANES)] = wide[c].reshape(devices, 8, LANES).astype(BF16)
    pl.semaphore_wait(barrier, devices - 1)

    def exchange(src, dst, n):
        def send(i, carry):
            p = lax.bitwise_and(me + i, devices - 1)
            pltpu.make_async_remote_copy(
                src.at[pl.ds(p, 1)],
                dst.at[pl.ds(me, 1)],
                send_sem.at[n],
                recv_sem.at[n],
                device_id=at_index(p),
                device_id_type=MESH,
            ).start()
            return carry

        lax.fori_loop(1, devices, send, 0)
        own = pltpu.make_async_copy(src.at[pl.ds(me, 1)], dst.at[pl.ds(me, 1)], self_sem.at[n])
        own.start()
        many = pl.ds(0, devices - 1)
        whole = pltpu.make_async_remote_copy(
            src.at[many],
            dst.at[many],
            send_sem.at[n],
            recv_sem.at[n],
            device_id=whom(cx, lax.rem(cz + 1, nz), cy),
            device_id_type=MESH,
        )
        return own, whole

    own, whole = exchange(ready, arrived, 0)

    for c in loads[3:8]:
        c.wait()
    for m, to in ((0, relu_f), (1, shrink_f)):
        for s in range(2):
            for j in range(4):
                blocks = []
                for kn in range(4):
                    k, n = divmod(kn, 2)
                    three = [
                        masks[m, 2 * s + n, pl.ds(2 * c + k, quarter, stride=6), :]
                        for c in range(3)
                    ]
                    blocks.append(moved(block_of(three, j), FIRST[j], FIRST[kn]))
                for c, v in enumerate(tiles_of(blocks)):
                    to[pl.ds(s * nlat + j * quarter, quarter), pl.ds(c * LANES, LANES)] = v.astype(
                        F32
                    )
    square[...] = jnp.zeros_like(square)
    weights[...] = jnp.zeros_like(weights)
    column = lane_of((WIDTH, LANES))
    for m, src in ((0, w_one_v), (1, w_two_v)):
        for t in range(2):
            for n in range(2):
                square[:, pl.ds(0, WIDTH)] = src[t, n].astype(F32)
                base = square[...]
                for k in range(2):
                    kn = 2 * k + n
                    turned = moved(base, 0, FIRST[kn])
                    rows = pl.ds(kn * WIDTH, WIDTH)
                    if kn < 3:
                        keep = column >= FIRST[kn] if kn else column < WIDTH
                        c = (0, 0, 1)[kn]
                        weights[2 * m + t, rows, pl.ds(c * LANES, LANES)] = jnp.where(
                            keep, turned, 0.0
                        ).astype(BF16)
                    if kn > 0:
                        keep = column >= FIRST[3] if kn == 3 else column < FIRST[kn + 1]
                        c = (0, 1, 2, 2)[kn]
                        weights[2 * m + t, rows, pl.ds(c * LANES, LANES)] = jnp.where(
                            keep, turned, 0.0
                        ).astype(BF16)
    for t in range(2):
        for n in range(2):
            bias_row[pl.ds(2 * t + n, 1), pl.ds(0, WIDTH)] = b_one_v[t, pl.ds(n, 1), :].astype(F32)
    for t in range(2):
        blocks = [
            moved(
                jnp.broadcast_to(bias_row[pl.ds(2 * t + kn % 2, 1), pl.ds(0, LANES)], (8, LANES)),
                0,
                FIRST[kn],
            )
            for kn in range(4)
        ]
        for c, v in enumerate(tiles_of(blocks)):
            bias_row[pl.ds(8 + 8 * t, 8), pl.ds(c * LANES, LANES)] = v

    for c in loads[8:10]:
        c.wait()
    own.wait()
    whole.wait_recv()
    stacked[...] = arrived[...].reshape(8 * devices, 384)
    chunk = min(256, nlat)
    for f in (1, 0):
        for a in range(0, 2 * nlat, chunk):
            rows = pl.ds(a, chunk)
            value = dot(north_v[pl.ds(2 * f * nlat + a, chunk), :], stacked[...]).astype(BF16)
            if f:
                upstream[rows, :] = (value.astype(F32) * shrink_f[rows, :]).astype(BF16)
            else:
                modes[rows, :] = value

    half = min(128, nlat)
    parts = [(pl.ds(a, half), pl.ds(nlat + a, half)) for a in range(0, nlat, half)]

    def conjugate_mix(src, top, low, m):
        a, b = (src[top, :], src[low, :])
        real = dot_turned(a, weights[2 * m]) + dot_turned(b, weights[2 * m + 1])
        imag = dot_turned(b, weights[2 * m]) - dot_turned(a, weights[2 * m + 1])
        return real, imag

    for top, low in parts:
        real, imag = conjugate_mix(upstream, top, low, 1)
        inner[top, :] = (relu_f[top, :] * real).astype(BF16)
        inner[low, :] = (relu_f[low, :] * imag).astype(BF16)
    for top, low in parts:
        a, b = (modes[top, :], modes[low, :])
        real = dot(a, weights[0]) - dot(b, weights[1]) + bias_row[pl.ds(8, 1), :]
        imag = dot(a, weights[1]) + dot(b, weights[0]) + bias_row[pl.ds(16, 1), :]
        hidden[top, :] = (relu_f[top, :] * real).astype(BF16)
        hidden[low, :] = (relu_f[low, :] * imag).astype(BF16)
    upper, lower = (pl.ds(0, nlat), pl.ds(nlat, nlat))

    def diagonal(product, n, start):
        total = None
        for k in range(2):
            kn = 2 * k + n
            rows = product[kn * WIDTH : (kn + 1) * WIDTH]
            tiles = [rows[:, c * LANES : (c + 1) * LANES] for c in range(3)]
            block = moved(block_of(tiles, kn), FIRST[kn], start)
            total = block if total is None else total + block
        return total

    eighth = WIDTH // 8
    for g, (left, right) in enumerate(((modes, inner), (hidden, upstream))):
        real = dot_rows(left[...], right[...])
        imag = dot_rows(left[upper, :], right[lower, :]) - dot_rows(left[lower, :], right[upper, :])
        blocks = [
            diagonal(product, n, FIRST[2 * t + n])
            for t, product in enumerate((real, imag))
            for n in range(2)
        ]
        for c, v in enumerate(tiles_of(blocks)):
            shared[pl.ds((3 * g + c) * eighth, eighth)] = v.reshape(eighth, 8, LANES).astype(BF16)
    row8 = lax.broadcasted_iota(jnp.int32, (8, LANES), 0)
    total = jnp.zeros((8, LANES), F32)
    for t in range(2):
        sums = jnp.sum(inner[pl.ds(t * nlat, nlat), :].astype(F32), axis=0, keepdims=True)
        tiles = [
            jnp.broadcast_to(sums[:, c * LANES : (c + 1) * LANES], (8, LANES)) for c in range(3)
        ]
        for n in range(2):
            value = moved(block_of(tiles, n), FIRST[n], 0) + moved(
                block_of(tiles, 2 + n), FIRST[2 + n], 0
            )
            total = jnp.where(row8 == 2 * t + n, value, total)
    shared[6 * eighth] = total.astype(BF16)

    def to_owner(i, carry):
        p = lax.rem(me + i, owners)

        @pl.when(p != me)
        def _():
            pltpu.make_async_remote_copy(
                shared.at[pl.ds(p * per_owner, per_owner)],
                own_sums.at[me],
                send_sem.at[2],
                recv_sem.at[2],
                device_id=at_index(p),
                device_id_type=MESH,
            ).start()

        return carry

    lax.fori_loop(0, owners, to_owner, 0)
    whole.wait_send()

    for top, low in parts:
        real, imag = conjugate_mix(inner, top, low, 0)
        grad_modes[top, :] = real.astype(BF16)
        grad_modes[low, :] = imag.astype(BF16)
    for a in range(0, 4 * devices, half):
        value = dot(turned_v[pl.ds(a, half), :], grad_modes[...]).astype(BF16)
        leaving[pl.ds(a // 4, half // 4)] = value.reshape(half // 4, 4, 384)

    own_back, whole_back = exchange(leaving, returned, 1)

    neighbour = whom(cx, lax.rem(cz + 1, nz), cy)

    def bytes_of(ref, n):
        return pltpu.make_async_remote_copy(
            ref,
            ref,
            send_sem.at[n],
            recv_sem.at[n],
            device_id=neighbour,
            device_id_type=MESH,
        )

    @pl.when(me < owners)
    def _():
        own_sums[me] = shared[pl.ds(me * per_owner, per_owner)]
        bytes_of(own_sums.at[pl.ds(0, devices - 1)], 2).wait_recv()
        all_sums[me] = jnp.sum(own_sums[...].astype(F32), axis=0).astype(BF16)

        def to_all(i, carry):
            pltpu.make_async_remote_copy(
                all_sums.at[me],
                all_sums.at[me],
                send_sem.at[3],
                recv_sem.at[3],
                device_id=at_index(lax.bitwise_and(me + i, devices - 1)),
                device_id_type=MESH,
            ).start()
            return carry

        lax.fori_loop(1, devices, to_all, 0)

    stores = [pltpu.make_async_copy(raw.at[0, h], out.at[h], load_sem.at[h]) for h in range(2)]
    loads[10].wait()
    own_back.wait()
    whole_back.wait_recv()
    back_rows[...] = returned[...].reshape(4 * devices, 384)
    for h in range(2):
        for j in range(4):
            rows = pl.ds(j * ROWS, ROWS)
            even = dot(back_v[h, 0, rows, :], back_rows[:, pl.ds(0, 256)])
            odd = dot(back_v[h, 1, rows, :], back_rows[:, pl.ds(128, 256)])
            tiles = (even[:, :128], even[:, 128:], None)
            parted = (None, odd[:, :128], odd[:, 128:])
            for n in range(2):
                value = moved(block_of(tiles, n), FIRST[n], FIRST[j]) + moved(
                    block_of(parted, 2 + n), FIRST[2 + n], FIRST[j]
                ) if n == 1 else moved(tiles[0], FIRST[0], FIRST[j]) + moved(
                    jnp.where(lane >= FIRST[2], parted[1], parted[2]), FIRST[2], FIRST[j]
                )
                result_out[j, n] = value
        for n in range(2):
            for c, v in enumerate(tiles_of([result_out[j, n] for j in range(4)])):
                result[h, pl.ds(2 * c + n, ROWS, stride=6), :] = v
        done = result[h, pl.ds(0, 6 * GROUPS), :] + raw[1, h].astype(F32)
        raw[0, h] = done.astype(BF16)
        stores[h].start()

    whole_back.wait_send()

    @pl.when(me < owners)
    def _():
        bytes_of(shared.at[pl.ds(0, (owners - 1) * per_owner)], 2).wait_send()
        bytes_of(own_sums.at[pl.ds(0, devices - 1)], 3).wait_send()
        bytes_of(all_sums.at[pl.ds(0, owners - 1)], 3).wait_recv()

    @pl.when(me >= owners)
    def _():
        bytes_of(shared.at[pl.ds(0, owners * per_owner)], 2).wait_send()
        bytes_of(all_sums.at[pl.ds(0, owners)], 3).wait_recv()

    for c in stores:
        c.wait()


def finish(
    factor,
    ahead,
    sums_in,
    out,
    first_out,
    bias_out,
    second_out,
    held,
    sums,
    first_v,
    bias_v,
    second_v,
    in_sem,
    out_sem,
):
    fetch = [
        pltpu.make_async_copy(src, dst, in_sem.at[i])
        for i, (src, dst) in enumerate(((ahead, held), (sums_in, sums)))
    ]
    store = [
        pltpu.make_async_copy(src, dst, out_sem.at[i])
        for i, (src, dst) in enumerate(
            ((held, out), (first_v, first_out), (second_v, second_out), (bias_v, bias_out))
        )
    ]
    for c in fetch:
        c.start()
    fetch[1].wait()
    eighth = WIDTH // 8
    for g, ref in enumerate((first_v, second_v)):
        tiles = [
            sums[pl.ds((3 * g + c) * eighth, eighth)].reshape(WIDTH, LANES).astype(F32)
            for c in range(3)
        ]
        for t in range(2):
            for n in range(2):
                i = 2 * t + n
                block = moved(block_of(tiles, i), FIRST[i], 0)
                ref[t, n] = block[:, :WIDTH] * factor
        if g == 0:
            fetch[0].wait()
            store[0].start()
        store[1 + g].start()
    last = sums[6 * eighth].astype(F32) * factor
    for t in range(2):
        bias_v[t] = last[2 * t : 2 * t + 2, :WIDTH]
    store[3].start()
    for c in store:
        c.wait()


def local(sizes, tokens, cotangent, first_weight, first_bias, second_weight, relu_mask, shrink_mask):
    devices = math.prod(sizes)
    nlat = 2 * devices
    blocks = 6 * WIDTH // 8 + 1
    per_owner = -(-blocks // devices)
    owners = -(-blocks // per_owner)

    pairs = Layout(major_to_minor=(0, 2, 1, 3))

    def in_rows(field):
        tiles = with_layout_constraint(field.reshape(2, 2, 3 * GROUPS, LANES), pairs)
        return tiles.transpose(0, 2, 1, 3).reshape(2, 6 * GROUPS, LANES)

    def mask_rows(mask):
        width = mask.shape[-1] // LANES
        return (
            mask.reshape(4, 2, width, LANES).transpose(0, 2, 1, 3).reshape(4, 2 * width, LANES)
        )

    constants = [jnp.asarray(t) for t in tables(devices)]
    anywhere = pl.BlockSpec(memory_space=pl.ANY)
    in_vmem = pl.BlockSpec(memory_space=pltpu.VMEM)

    def vmem(*shape, dtype=BF16):
        return pltpu.VMEM(shape, dtype)

    ahead, sums = pl.pallas_call(
        functools.partial(kernel, sizes, per_owner, owners),
        out_shape=(
            jax.ShapeDtypeStruct((2, 6 * GROUPS, LANES), BF16),
            jax.ShapeDtypeStruct((owners, per_owner, 8, LANES), BF16),
        ),
        in_specs=[anywhere] * 11,
        out_specs=(anywhere, in_vmem),
        scratch_shapes=[
            vmem(2, 2, 6 * GROUPS, LANES),
            vmem(4, 6 * ROWS, LANES, dtype=F32),
            vmem(4, 4 * ROWS, 4 * LANES),
            vmem(3, 8 * devices, LANES, dtype=F32),
            vmem(devices, 8, 384),
            vmem(devices, 8, 384),
            vmem(8 * devices, 384),
            vmem(2, 4, 6 * (nlat // 4), LANES, dtype=jnp.int32),
            vmem(2 * nlat, 384, dtype=F32),
            vmem(2 * nlat, 384, dtype=F32),
            vmem(4, 384, 384),
            vmem(WIDTH, LANES, dtype=F32),
            vmem(24, 384, dtype=F32),
            vmem(2 * nlat, 384),
            vmem(2 * nlat, 384),
            vmem(2 * nlat, 384),
            vmem(2 * nlat, 384),
            vmem(2 * nlat, 384),
            vmem(devices, 4, 384),
            vmem(devices, 4, 384),
            vmem(4 * devices, 384),
            vmem(devices, per_owner, 8, LANES),
            vmem(owners * per_owner, 8, LANES),
            vmem(2, 6 * ROWS, LANES, dtype=F32),
            vmem(4, 2, ROWS, LANES, dtype=F32),
            vmem(*constants[0].shape),
            vmem(*constants[1].shape),
            vmem(*constants[2].shape),
            vmem(*constants[3].shape),
            vmem(*first_weight.shape),
            vmem(*first_bias.shape),
            vmem(*second_weight.shape),
            pltpu.SemaphoreType.DMA((11,)),
            pltpu.SemaphoreType.DMA((2,)),
            pltpu.SemaphoreType.DMA((4,)),
            pltpu.SemaphoreType.DMA((4,)),
        ],
        compiler_params=pltpu.CompilerParams(
            collective_id=0, has_side_effects=True, vmem_limit_bytes=60 * 1024 * 1024
        ),
    )(
        in_rows(tokens),
        in_rows(cotangent),
        first_weight,
        first_bias,
        second_weight,
        mask_rows(relu_mask),
        mask_rows(shrink_mask),
        *constants,
    )
    out, first, bias, second = pl.pallas_call(
        functools.partial(finish, 1.0 / math.sqrt(nlat * 2 * devices)),
        out_shape=(
            jax.ShapeDtypeStruct((2, 6 * GROUPS, LANES), BF16),
            jax.ShapeDtypeStruct(first_weight.shape, F32),
            jax.ShapeDtypeStruct(first_bias.shape, F32),
            jax.ShapeDtypeStruct(second_weight.shape, F32),
        ),
        in_specs=(anywhere, anywhere),
        out_specs=(anywhere,) * 4,
        scratch_shapes=[
            vmem(2, 6 * GROUPS, LANES),
            vmem(owners * per_owner, 8, LANES),
            vmem(*first_weight.shape, dtype=F32),
            vmem(*first_bias.shape, dtype=F32),
            vmem(*second_weight.shape, dtype=F32),
            pltpu.SemaphoreType.DMA((2,)),
            pltpu.SemaphoreType.DMA((4,)),
        ],
    )(ahead, sums.reshape(owners * per_owner, 8, LANES))
    out = out.reshape(2, 3 * GROUPS, 2, LANES).transpose(0, 2, 1, 3)
    token_gradient = with_layout_constraint(out, pairs).reshape(tokens.shape)
    return (token_gradient, first, bias, second)


def solution(mesh, sizes=(4, 8, 4)):
    finer = Mesh(mesh.devices.reshape(*sizes, mesh.shape["ch"]), (*NAMES, "ch"))
    in_specs = (
        P(None, NAMES, "ch", None),
        P(None, NAMES, "ch", None),
        P(None, "ch", None, None),
        P(None, "ch", None),
        P(None, "ch", None, None),
        P(None, None, "ch", NAMES, None),
        P(None, None, "ch", NAMES, None),
    )
    out_specs = (
        P(None, NAMES, "ch", None),
        P(None, "ch", None, None),
        P(None, "ch", None),
        P(None, "ch", None, None),
    )
    return jax.shard_map(
        functools.partial(local, sizes),
        mesh=finer,
        in_specs=in_specs,
        out_specs=out_specs,
        check_vma=False,
    )
```
